128 devices in a mesh: grp: 16 (over x, z), mem: 8 (over y, core).
Axes of the slice: x: 4, y: 4, z: 4, core: 2. Of those that a mesh axis runs over, the one named last changes fastest.
Arguments:
- hidden: bfloat16 [262144, 256], P(('grp', 'mem')), may hold values from -6 to 6
- initial: bfloat16 [262144, 256], P(('grp', 'mem')), may hold values from -6 to 6
- weight: bfloat16 [256, 256], replicated, may hold values from -0.375 to 0.375
- grp_vals: bfloat16 [28672, 128, 128], P(('grp', 'mem')), may hold values from -0.125 to 0.125
- grp_row: int32 [28672], P(('grp', 'mem')), may hold values from 0 to 15
- grp_col: int32 [28672], P(('grp', 'mem')), may hold values from 0 to 127
- bnd_vals: bfloat16 [14336, 128, 128], P(('grp', 'mem')), may hold values from -0.125 to 0.125
- bnd_src: int32 [14336], P(('grp', 'mem')), may hold values from 0 to 15
- bnd_dst: int32 [14336, 1], P(('grp', 'mem')), may hold values from 0 to 127; in each aligned block of 112 rows (0 to 111, 112 to 223, ...) at most 2 rows name the same one
- bnd_row: int32 [14336], P(('grp', 'mem')), may hold values from 0 to 15
- cotangent: bfloat16 [262144, 256], P(('grp', 'mem')), may hold values from -6 to 6
Outputs:
- output: bfloat16 [262144, 256], P(('grp', 'mem'))
- grad_weight: float32 [256, 256], replicated
- grad_hidden: bfloat16 [262144, 256], P(('grp', 'mem'))
The draws below stay inside these ranges and needn't reach their ends.
Inputs may be any that keep to these rules, and one draw needn't show every extreme that they name: `bnd_dst`: among the boundary edge blocks of one device, at most 2 name any one device, and on some device exactly 2 name one device.
All inputs are finite; a program needn't handle non-finite values.
Results may differ from the reference program's by a relative error of at most 0.017.
Values may be sent and summed in bfloat16 or wider, within the bound.
A program may use at most 256 MiB of HBM per device.

```python
import math
import jax
import jax.numpy as jnp
import numpy as np
from jax import lax

F = 256
BLK = 128
NB = 16
EPB = 14
GB = 224
BB = 112
CAP = 2
NODES = 262144
N_GRP = 16
N_MEM = 8
DEVICES = 128


def with_ends(result, key, least, largest):
    spot = [jax.random.randint(jax.random.fold_in(key, axis), (), 0, length) for axis, length in enumerate(result.shape)]
    widest = result.shape.index(max(result.shape))
    beside = spot[:widest] + [(spot[widest] + 1) % result.shape[widest]] + spot[widest + 1:]
    return result.at[tuple(spot)].set(least).at[tuple(beside)].set(largest)


def shard_levels(own_key, dims, pieces, smallest, high):
    def one(axis_at, parts):
        steps = jax.random.uniform(jax.random.fold_in(jax.random.fold_in(own_key, 6), axis_at), (parts,), jnp.float32, smallest / len(pieces), high / len(pieces))
        return jnp.repeat(jnp.exp(steps), dims[axis_at] // parts).reshape((-1,) + (1,) * (len(dims) - axis_at - 1))

    level = one(*pieces[0])
    for cut in pieces[1:]:
        level = level * one(*cut)
    return level


def assign_block(own_key, own, number, rows, count, top, most, skew):
    ranking = jax.random.permutation(own_key, count)
    crowded, ordinary = load_shares(count, rows * top, most, skew, True), load_shares(count, rows * top, most, skew, False)
    places = jnp.arange(count)

    def named(lengths, rotation):
        used = int((lengths > 0).sum())
        fixed = max(1, used // 4)
        passed = fixed + (places - fixed + rotation * (used - fixed)) % max(1, count - fixed)
        return jnp.zeros((count,), jnp.int32).at[ranking[jnp.where(places < fixed, places, passed)]].set(jnp.asarray(lengths, jnp.int32))

    lengths = jnp.where(number % 4 == 0, named(crowded, number // 4), named(ordinary, number - number // 4 - 1))
    mixed = jax.random.permutation(jax.random.fold_in(own, 3), count)
    source_of, taker = mixed[0:count // 2 * 2:2], mixed[1:count // 2 * 2:2]
    room = jnp.minimum(lengths[source_of] - 1, most - lengths[taker]) // 2
    room = jnp.where((source_of == ranking[0]) | (taker == ranking[0]) | (lengths[taker] == 0), 0, jnp.maximum(room, 0))
    passed = jax.random.randint(jax.random.fold_in(own, 4), (count // 2,), 0, 1 << 20) % (room + 1)
    lengths = lengths.at[source_of].add(-passed).at[taker].add(passed)
    members = jnp.searchsorted(jnp.cumsum(lengths), jnp.arange(rows * top), side="right").astype(jnp.int32)
    table = members.reshape(top, rows).T
    table = table[jax.random.permutation(jax.random.fold_in(own, 1), rows)]
    rotation = jax.random.randint(jax.random.fold_in(own, 2), (rows, 1), 0, top)
    return jnp.take_along_axis(table, (jnp.arange(top)[None, :] + rotation) % top, axis=1)


def load_shares(count, total, most, slope, full):
    loads = [(1 << 20) // math.isqrt(rank ** slope) + 1 for rank in range(1, count + 1)]
    largest = most if full else min(most, max(-(-total // count), total * loads[0] // sum(loads)))
    least = 1 if total - largest >= count - 1 else 0
    counts, spare = [largest] + [least] * (count - 1), total - largest - least * (count - 1)
    while spare > 0:
        candidates = [i for i in range(1, count) if counts[i] < largest] or [i for i in range(1, count) if counts[i] < most]
        mass, left = sum([loads[i] for i in candidates]), spare
        for i in candidates:
            more = min(most - counts[i], max(1, left * loads[i] // mass), spare)
            counts[i] = counts[i] + more
            spare = spare - more
    return np.array(counts)


def gaussian(own_key, shape, deviation, limit, cuts=(), kind=jnp.bfloat16):
    values = deviation * jax.random.normal(own_key, shape, jnp.float32)
    if cuts:
        values = values * shard_levels(own_key, shape, cuts, -0.22, 0.18)
    return jnp.clip(values, -limit, limit).astype(kind)


def setup_inputs(seed: int = 0) -> dict:
    key_of = jax.random.split(jax.random.key(seed), 12)
    hidden = gaussian(key_of[0], (NODES, F), 1.0, 6.0, ((0, 128),))
    initial = gaussian(key_of[1], (NODES, F), 1.0, 6.0, ((0, 128),))
    weight = gaussian(key_of[2], (F, F), F ** -0.5, 0.375)
    grp_vals = gaussian(key_of[3], (DEVICES * GB, BLK, BLK), (BLK * (EPB + 7)) ** -0.5, 0.125, ((0, 128),))
    grp_row = with_ends(jax.random.randint(key_of[4], (DEVICES * GB,), 0, NB), jax.random.fold_in(key_of[4], 1), 0, NB - 1).astype(jnp.int32)
    grp_col = with_ends(jax.random.randint(key_of[5], (DEVICES * GB,), 0, N_MEM * NB), jax.random.fold_in(key_of[5], 1), 0, (N_MEM * NB) - 1).astype(jnp.int32)
    bnd_vals = gaussian(key_of[6], (DEVICES * BB, BLK, BLK), (BLK * (EPB + 7)) ** -0.5, 0.125, ((0, 128),))
    bnd_src = with_ends(jax.random.randint(key_of[7], (DEVICES * BB,), 0, NB), jax.random.fold_in(key_of[7], 1), 0, NB - 1).astype(jnp.int32)
    bnd_dst_keys = jax.random.split(jax.random.fold_in(key_of[8], 1), (DEVICES * BB) // BB)
    bnd_dst_turns = jax.random.permutation(jax.random.fold_in(key_of[8], 3), (DEVICES * BB) // BB)
    bnd_dst = jax.vmap(lambda own, number: assign_block(jax.random.fold_in(key_of[8], 2), own, number, BB, DEVICES, 1, CAP, 2))(bnd_dst_keys, bnd_dst_turns).reshape((DEVICES * BB, 1))
    bnd_row = with_ends(jax.random.randint(key_of[9], (DEVICES * BB,), 0, NB), jax.random.fold_in(key_of[9], 1), 0, NB - 1).astype(jnp.int32)
    cotangent = gaussian(key_of[10], (NODES, F), 1.0, 6.0, ((0, 128),))
    return {"hidden": hidden, "initial": initial, "weight": weight, "grp_vals": grp_vals, "grp_row": grp_row, "grp_col": grp_col, "bnd_vals": bnd_vals, "bnd_src": bnd_src, "bnd_dst": bnd_dst, "bnd_row": bnd_row, "cotangent": cotangent}


def reference(hidden, initial, weight, grp_vals, grp_row, grp_col, bnd_vals, bnd_src, bnd_dst, bnd_row, cotangent):
    devices = N_GRP * N_MEM
    blocks = hidden.reshape(devices * NB, BLK, F)
    indices = jnp.arange(devices, dtype=jnp.int32)
    group_vals = grp_vals.reshape(devices, GB, BLK, BLK)
    group_rows = grp_row.reshape(devices, GB)
    group_cols = grp_col.reshape(devices, GB)
    edge_vals = bnd_vals.reshape(devices, BB, BLK, BLK)
    sources = bnd_src.reshape(devices, BB)
    targets = bnd_dst.reshape(devices, BB)
    target_rows = bnd_row.reshape(devices, BB)

    def forward_device(summed, inputs):
        device, vals, rows, cols, bvals, srcs, dsts, drows = inputs
        group_start = device // N_MEM * (N_MEM * NB)
        picked = blocks[group_start + cols].astype(jnp.float32)
        messages = jnp.einsum('bij,bjf->bif', vals.astype(jnp.float32), picked)
        summed = summed.at[device * NB + rows].add(messages)
        own = blocks[device * NB + srcs].astype(jnp.float32)
        partial_value = jnp.einsum('bij,bjf->bif', bvals.astype(jnp.float32), own).astype(jnp.bfloat16)
        partial_value = lax.optimization_barrier(partial_value).astype(jnp.float32)
        summed = summed.at[dsts * NB + drows].add(partial_value)
        return (summed, None)
    summed, _ = lax.scan(forward_device, jnp.zeros((devices * NB, BLK, F), jnp.float32), (indices, group_vals, group_rows, group_cols, edge_vals, sources, targets, target_rows))
    mixed = (0.9 * summed.reshape(-1, F) + 0.1 * initial.astype(jnp.float32)).astype(jnp.bfloat16)
    mix_weight = (0.5 * jnp.eye(F, dtype=jnp.float32) + 0.5 * weight.astype(jnp.float32)).astype(jnp.bfloat16)
    pre = jnp.dot(mixed, mix_weight, preferred_element_type=jnp.float32)
    output = jax.nn.silu(pre).astype(jnp.bfloat16)
    sigmoid_pre = jax.nn.sigmoid(pre)
    grad_pre = (cotangent.astype(jnp.float32) * sigmoid_pre * (1.0 + pre * (1.0 - sigmoid_pre))).astype(jnp.bfloat16)
    grad_weight = 0.5 * jnp.dot(mixed.T, grad_pre, preferred_element_type=jnp.float32) / math.sqrt(NODES)
    grad_mixed = jnp.dot(grad_pre, mix_weight.T, preferred_element_type=jnp.float32).astype(jnp.bfloat16)
    grad_blocks = grad_mixed.reshape(devices * NB, BLK, F)

    def backward_device(accum, inputs):
        device, vals, rows, cols = inputs
        group_start = device // N_MEM * (N_MEM * NB)
        upstream = grad_blocks[device * NB + rows].astype(jnp.float32)
        transposed = jnp.einsum('bji,bjf->bif', vals.astype(jnp.float32), upstream)
        term = jnp.zeros((N_MEM * NB, BLK, F), jnp.float32).at[cols].add(transposed)
        term = (0.9 * term).astype(jnp.bfloat16)
        term = lax.optimization_barrier(term).astype(jnp.float32)
        current = lax.dynamic_slice_in_dim(accum, group_start, N_MEM * NB, 0)
        accum = lax.dynamic_update_slice_in_dim(accum, current + term, group_start, 0)
        return (accum, None)
    accum, _ = lax.scan(backward_device, jnp.zeros((devices * NB, BLK, F), jnp.float32), (indices, group_vals, group_rows, group_cols))
    grad_hidden = accum.reshape(-1, F).astype(jnp.bfloat16)
    return (output, grad_weight, grad_hidden)
```

```python
import math

import jax
import jax.numpy as jnp
from jax import lax
from jax.experimental import pallas as pl
from jax.experimental.pallas import tpu as pltpu
from jax.sharding import PartitionSpec as P

AXES = ("grp", "mem")
VMEM_LIMIT = 56 * 1024 * 1024


def params(**kw):
    return pltpu.CompilerParams(vmem_limit_bytes=VMEM_LIMIT, **kw)


def full(shape):
    return pl.BlockSpec(shape, lambda *_: (0,) * len(shape))


def cost(flops, moved):
    return pl.CostEstimate(flops=flops, bytes_accessed=moved, transcendentals=0)


def partial_kernel(edge_ref, src_ref, vals_ref, hid_ref, out_ref):
    step = pl.program_id(0)
    per_step = out_ref.shape[0]
    blk = vals_ref.shape[1]
    for i in range(per_step):
        for k in range(2):
            edge = edge_ref[(step * per_step + i) * 2 + k]

            @pl.when(edge >= 0)
            def _():
                out_ref[i, k * blk : (k + 1) * blk, :] = jnp.dot(
                    vals_ref[edge], hid_ref[src_ref[edge]], preferred_element_type=jnp.float32
                ).astype(out_ref.dtype)


def partials(slot_edge, bnd_src, bnd_vals, blocks, devices):
    count, blk, _ = bnd_vals.shape
    nb, _, feat = blocks.shape
    per_step = 4
    return pl.pallas_call(
        partial_kernel,
        grid_spec=pltpu.PrefetchScalarGridSpec(
            num_scalar_prefetch=2,
            grid=(devices // per_step,),
            in_specs=[full(bnd_vals.shape), full(blocks.shape)],
            out_specs=pl.BlockSpec((per_step, 2 * blk, feat), lambda i, *_: (i, 0, 0)),
        ),
        out_shape=jax.ShapeDtypeStruct((devices, 2 * blk, feat), jnp.bfloat16),
        compiler_params=params(),
        cost_estimate=cost(2 * count * blk * blk * feat, devices * 4 * blk * feat),
    )(slot_edge, bnd_src, bnd_vals, blocks)


def forward_kernel(row_ref, col_ref, vals_ref, table_ref, out_ref):
    step = pl.program_id(0)
    per_step = vals_ref.shape[0]

    @pl.when(step == 0)
    def _():
        out_ref[...] = jnp.zeros_like(out_ref)

    for i in range(per_step):
        b = step * per_step + i
        row = row_ref[b]
        out_ref[row] += jnp.dot(
            vals_ref[i], table_ref[col_ref[b]], preferred_element_type=jnp.float32
        )


def group_forward(grp_row, grp_col, grp_vals, table, nb):
    count, blk, _ = grp_vals.shape
    feat = table.shape[-1]
    per_step = 16
    return pl.pallas_call(
        forward_kernel,
        grid_spec=pltpu.PrefetchScalarGridSpec(
            num_scalar_prefetch=2,
            grid=(count // per_step,),
            in_specs=[
                pl.BlockSpec((per_step, blk, blk), lambda i, *_: (i, 0, 0)),
                full(table.shape),
            ],
            out_specs=full((nb, blk, feat)),
        ),
        out_shape=jax.ShapeDtypeStruct((nb, blk, feat), jnp.float32),
        compiler_params=params(),
        cost_estimate=cost(2 * count * blk * blk * feat, 40_000_000),
    )(grp_row, grp_col, grp_vals, table)


def mid_kernel(
    total_nodes,
    rows_ref,
    inc_ref,
    summed_ref,
    initial_ref,
    cot_ref,
    w_ref,
    out_ref,
    gmix_ref,
    gw_ref,
    acc,
    mw,
):
    step = pl.program_id(0)
    per_step = inc_ref.shape[0]
    nb, blk, feat = acc.shape

    @pl.when(step == 0)
    def _():
        acc[...] = summed_ref[...]

    for i in range(per_step):
        for k in range(2):
            row = rows_ref[(step * per_step + i) * 2 + k]

            @pl.when(row >= 0)
            def _():
                acc[row] += inc_ref[i, k * blk : (k + 1) * blk, :].astype(jnp.float32)

    @pl.when(step == pl.num_programs(0) - 1)
    def _():
        eye = lax.broadcasted_iota(jnp.int32, (feat, feat), 0) == lax.broadcasted_iota(
            jnp.int32, (feat, feat), 1
        )
        mw[...] = (
            jnp.where(eye, 0.5, 0.0).astype(jnp.float32) + 0.5 * w_ref[...].astype(jnp.float32)
        ).astype(jnp.bfloat16)
        gw_ref[...] = jnp.zeros_like(gw_ref)

        def body(j, _):
            at = pl.ds(pl.multiple_of(j * blk, blk), blk)
            mixed = (0.9 * acc[j] + 0.1 * initial_ref[at, :].astype(jnp.float32)).astype(
                jnp.bfloat16
            )
            pre = jnp.dot(mixed, mw[...], preferred_element_type=jnp.float32)
            sig = jax.nn.sigmoid(pre)
            out_ref[at, :] = (pre * sig).astype(jnp.bfloat16)
            gpre = (cot_ref[at, :].astype(jnp.float32) * sig * (1.0 + pre * (1.0 - sig))).astype(
                jnp.bfloat16
            )
            gw_ref[...] += lax.dot_general(
                mixed, gpre, (((0,), (0,)), ((), ())), preferred_element_type=jnp.float32
            )
            gmix_ref[at, :] = lax.dot_general(
                gpre, mw[...], (((1,), (1,)), ((), ())), preferred_element_type=jnp.float32
            ).astype(jnp.bfloat16)
            return 0

        lax.fori_loop(0, nb, body, 0)


def middle(in_rows, incoming, summed, initial, cotangent, weight, total_nodes):
    devices, two_blk, feat = incoming.shape
    nb, blk, _ = summed.shape
    nodes = nb * blk
    per_step = 8
    return pl.pallas_call(
        lambda *refs: mid_kernel(total_nodes, *refs),
        grid_spec=pltpu.PrefetchScalarGridSpec(
            num_scalar_prefetch=1,
            grid=(devices // per_step,),
            in_specs=[
                pl.BlockSpec((per_step, two_blk, feat), lambda i, *_: (i, 0, 0)),
                full(summed.shape),
                full(initial.shape),
                full(cotangent.shape),
                full(weight.shape),
            ],
            out_specs=[full((nodes, feat)), full((nodes, feat)), full((feat, feat))],
            scratch_shapes=[
                pltpu.VMEM((nb, blk, feat), jnp.float32),
                pltpu.VMEM((feat, feat), jnp.bfloat16),
            ],
        ),
        out_shape=[
            jax.ShapeDtypeStruct((nodes, feat), jnp.bfloat16),
            jax.ShapeDtypeStruct((nodes, feat), jnp.bfloat16),
            jax.ShapeDtypeStruct((feat, feat), jnp.float32),
        ],
        compiler_params=params(),
        cost_estimate=cost(6 * nodes * feat * feat, 30_000_000),
    )(in_rows, incoming, summed, initial, cotangent, weight)


def backward_kernel(row_ref, col_ref, vals_ref, gmix_ref, out_ref, acc):
    step = pl.program_id(0)
    per_step = vals_ref.shape[0]

    @pl.when(step == 0)
    def _():
        def zero(j, _):
            acc[j] = jnp.zeros(acc.shape[1:], acc.dtype)
            return 0

        lax.fori_loop(0, acc.shape[0], zero, 0)

    for i in range(per_step):
        b = step * per_step + i
        col = col_ref[b]
        acc[col] += lax.dot_general(
            vals_ref[i],
            gmix_ref[row_ref[b]],
            (((0,), (0,)), ((), ())),
            preferred_element_type=jnp.float32,
        )

    @pl.when(step == pl.num_programs(0) - 1)
    def _():
        def write(j, _):
            out_ref[j] = (0.9 * acc[j]).astype(out_ref.dtype)
            return 0

        lax.fori_loop(0, acc.shape[0], write, 0)


def group_backward(grp_row, grp_col, grp_vals, gmix, members):
    count, blk, _ = grp_vals.shape
    nb, _, feat = gmix.shape
    per_step = 16
    return pl.pallas_call(
        backward_kernel,
        grid_spec=pltpu.PrefetchScalarGridSpec(
            num_scalar_prefetch=2,
            grid=(count // per_step,),
            in_specs=[
                pl.BlockSpec((per_step, blk, blk), lambda i, *_: (i, 0, 0)),
                full(gmix.shape),
            ],
            out_specs=full((nb * members, blk, feat)),
            scratch_shapes=[pltpu.VMEM((nb * members, blk, feat), jnp.float32)],
        ),
        out_shape=jax.ShapeDtypeStruct((nb * members, blk, feat), jnp.bfloat16),
        compiler_params=params(),
        cost_estimate=cost(2 * count * blk * blk * feat, 40_000_000),
    )(grp_row, grp_col, grp_vals, gmix)


def first_and_last(mask, key, axis):
    big = jnp.int32(1 << 30)
    low = jnp.min(jnp.where(mask, key, big), axis=axis)
    high = jnp.max(jnp.where(mask, key, -1), axis=axis)
    return jnp.where(low == big, -1, low), jnp.where(high == low, -1, high)


def per_device(
    hidden,
    initial,
    weight,
    grp_vals,
    grp_row,
    grp_col,
    bnd_vals,
    bnd_src,
    bnd_dst,
    bnd_row,
    cotangent,
):
    blk = grp_vals.shape[1]
    nodes, feat = hidden.shape
    nb = nodes // blk
    devices = lax.axis_size(AXES)
    members = lax.axis_size("mem")
    count = bnd_vals.shape[0]
    me = lax.axis_index(AXES)
    blocks = hidden.reshape(nb, blk, feat)

    target = bnd_dst[:, 0]
    ids = jnp.arange(count, dtype=jnp.int32)
    slot_edge = jnp.stack(
        first_and_last(
            target[None, :] == jnp.arange(devices, dtype=jnp.int32)[:, None],
            jnp.broadcast_to(ids[None, :], (devices, count)),
            1,
        ),
        axis=1,
    ).reshape(-1)
    table = lax.all_gather(blocks, "mem", axis=0, tiled=True)
    codes = lax.all_gather(target * nb + bnd_row, AXES, axis=0, tiled=False)

    outgoing = partials(slot_edge, bnd_src, bnd_vals, blocks, devices)
    incoming = lax.all_to_all(outgoing, AXES, split_axis=0, concat_axis=0, tiled=True)
    summed = group_forward(grp_row, grp_col, grp_vals, table, nb)

    low, high = first_and_last(codes // nb == me, ids[None, :] * nb + codes % nb, 1)
    in_rows = jnp.stack(
        [jnp.where(low < 0, -1, low % nb), jnp.where(high < 0, -1, high % nb)], axis=1
    ).reshape(-1)

    output, gmix, local_weight = middle(
        in_rows, incoming, summed, initial, cotangent, weight, nodes * devices
    )
    grad_weight = 0.5 * lax.psum(local_weight, AXES) / math.sqrt(nodes * devices)
    term = group_backward(grp_row, grp_col, grp_vals, gmix.reshape(nb, blk, feat), members)
    grad_table = lax.psum_scatter(term, "mem", scatter_dimension=0, tiled=True)
    return output, grad_weight, grad_table.reshape(nodes, feat)


def solution(mesh):
    return jax.shard_map(
        per_device,
        mesh=mesh,
        in_specs=(
            P(AXES, None),
            P(AXES, None),
            P(),
            P(AXES, None, None),
            P(AXES),
            P(AXES),
            P(AXES, None, None),
            P(AXES),
            P(AXES, None),
            P(AXES),
            P(AXES, None),
        ),
        out_specs=(P(AXES, None), P(), P(AXES, None)),
        check_vma=False,
    )
```

```python
import math

import jax
import jax.numpy as jnp
from jax import lax
from jax.experimental import pallas as pl
from jax.experimental.pallas import tpu as pltpu
from jax.sharding import PartitionSpec as P

AXES = ("grp", "mem")
MESH = pl.DeviceIdType.MESH
VMEM_LIMIT = 56 * 1024 * 1024


def params(**kw):
    return pltpu.CompilerParams(vmem_limit_bytes=VMEM_LIMIT, **kw)


def full(shape):
    return pl.BlockSpec(shape, lambda *_: (0,) * len(shape))


def cost(flops, moved):
    return pl.CostEstimate(flops=flops, bytes_accessed=moved, transcendentals=0)


def partial_kernel(slot_ref, src_ref, vals_ref, hid_ref, out_ref, stage, sem):
    step = pl.program_id(0)
    half = lax.rem(step, 2)
    per_step = vals_ref.shape[0]

    def drain(which):
        for i in range(per_step):
            pltpu.make_async_copy(stage.at[which, i], out_ref.at[0], sem.at[which, i]).wait()

    @pl.when(step >= 2)
    def _():
        drain(half)

    for i in range(per_step):
        edge = step * per_step + i
        stage[half, i] = jnp.dot(
            vals_ref[i], hid_ref[src_ref[edge]], preferred_element_type=jnp.float32
        ).astype(stage.dtype)
    for i in range(per_step):
        edge = step * per_step + i
        pltpu.make_async_copy(
            stage.at[half, i], out_ref.at[slot_ref[edge]], sem.at[half, i]
        ).start()

    @pl.when(step == pl.num_programs(0) - 1)
    def _():
        drain(1 - half)
        drain(half)


def partials(slot, bnd_src, bnd_vals, blocks, devices):
    count, blk, _ = bnd_vals.shape
    nb, _, feat = blocks.shape
    per_step = 8
    assert count % per_step == 0 and count >= 2 * per_step
    return pl.pallas_call(
        partial_kernel,
        grid_spec=pltpu.PrefetchScalarGridSpec(
            num_scalar_prefetch=2,
            grid=(count // per_step,),
            in_specs=[
                pl.BlockSpec((per_step, blk, blk), lambda i, *_: (i, 0, 0)),
                full(blocks.shape),
            ],
            out_specs=pl.BlockSpec(memory_space=pl.ANY),
            scratch_shapes=[
                pltpu.VMEM((2, per_step, blk, feat), jnp.bfloat16),
                pltpu.SemaphoreType.DMA((2, per_step)),
            ],
        ),
        out_shape=jax.ShapeDtypeStruct((devices * 2, blk, feat), jnp.bfloat16),
        compiler_params=params(),
        cost_estimate=cost(2 * count * blk * blk * feat, 3 * count * blk * feat),
    )(slot, bnd_src, bnd_vals, blocks)


def forward_kernel(row_ref, col_ref, vals_ref, table_ref, out_ref):
    step = pl.program_id(0)
    per_step = vals_ref.shape[0]

    @pl.when(step == 0)
    def _():
        out_ref[...] = jnp.zeros_like(out_ref)

    for i in range(per_step):
        b = step * per_step + i
        row = row_ref[b]
        out_ref[row] += jnp.dot(
            vals_ref[i], table_ref[col_ref[b]], preferred_element_type=jnp.float32
        )


def group_forward(grp_row, grp_col, grp_vals, table, nb):
    count, blk, _ = grp_vals.shape
    feat = table.shape[-1]
    per_step = 16
    return pl.pallas_call(
        forward_kernel,
        grid_spec=pltpu.PrefetchScalarGridSpec(
            num_scalar_prefetch=2,
            grid=(count // per_step,),
            in_specs=[
                pl.BlockSpec((per_step, blk, blk), lambda i, *_: (i, 0, 0)),
                full(table.shape),
            ],
            out_specs=full((nb, blk, feat)),
        ),
        out_shape=jax.ShapeDtypeStruct((nb, blk, feat), jnp.float32),
        compiler_params=params(),
        cost_estimate=cost(2 * count * blk * blk * feat, 40_000_000),
    )(grp_row, grp_col, grp_vals, table)


def mid_kernel(
    total_nodes,
    rows_ref,
    inc_ref,
    summed_ref,
    initial_ref,
    cot_ref,
    w_ref,
    out_ref,
    gmix_ref,
    gw_ref,
    acc,
    mw,
):
    step = pl.program_id(0)
    per_step = inc_ref.shape[0]
    nb, blk, feat = acc.shape

    @pl.when(step == 0)
    def _():
        acc[...] = summed_ref[...]

    for i in range(per_step):
        for k in range(2):
            row = rows_ref[(step * per_step + i) * 2 + k]

            @pl.when(row >= 0)
            def _():
                acc[row] += inc_ref[i, k * blk : (k + 1) * blk, :].astype(jnp.float32)

    @pl.when(step == pl.num_programs(0) - 1)
    def _():
        eye = lax.broadcasted_iota(jnp.int32, (feat, feat), 0) == lax.broadcasted_iota(
            jnp.int32, (feat, feat), 1
        )
        mw[...] = (
            jnp.where(eye, 0.5, 0.0).astype(jnp.float32) + 0.5 * w_ref[...].astype(jnp.float32)
        ).astype(jnp.bfloat16)
        gw_ref[...] = jnp.zeros_like(gw_ref)

        tall = 2 * blk

        def body(j, _):
            at = pl.ds(pl.multiple_of(j * tall, tall), tall)
            summed = acc[pl.ds(2 * j, 2)].reshape(tall, feat)
            mixed = (0.9 * summed + 0.1 * initial_ref[at, :].astype(jnp.float32)).astype(
                jnp.bfloat16
            )
            pre = jnp.dot(mixed, mw[...], preferred_element_type=jnp.float32)
            sig = jax.nn.sigmoid(pre)
            out_ref[at, :] = (pre * sig).astype(jnp.bfloat16)
            gpre = (cot_ref[at, :].astype(jnp.float32) * sig * (1.0 + pre * (1.0 - sig))).astype(
                jnp.bfloat16
            )
            gw_ref[...] += lax.dot_general(
                mixed, gpre, (((0,), (0,)), ((), ())), preferred_element_type=jnp.float32
            )
            gmix_ref[at, :] = lax.dot_general(
                gpre, mw[...], (((1,), (1,)), ((), ())), preferred_element_type=jnp.float32
            ).astype(jnp.bfloat16)
            return 0

        lax.fori_loop(0, nb // 2, body, 0)


def middle(in_rows, incoming, summed, initial, cotangent, weight, total_nodes):
    devices, two_blk, feat = incoming.shape
    nb, blk, _ = summed.shape
    nodes = nb * blk
    per_step = 8
    return pl.pallas_call(
        lambda *refs: mid_kernel(total_nodes, *refs),
        grid_spec=pltpu.PrefetchScalarGridSpec(
            num_scalar_prefetch=1,
            grid=(devices // per_step,),
            in_specs=[
                pl.BlockSpec((per_step, two_blk, feat), lambda i, *_: (i, 0, 0)),
                full(summed.shape),
                full(initial.shape),
                full(cotangent.shape),
                full(weight.shape),
            ],
            out_specs=[full((nodes, feat)), full((nodes, feat)), full((feat, feat))],
            scratch_shapes=[
                pltpu.VMEM((nb, blk, feat), jnp.float32),
                pltpu.VMEM((feat, feat), jnp.bfloat16),
            ],
        ),
        out_shape=[
            jax.ShapeDtypeStruct((nodes, feat), jnp.bfloat16),
            jax.ShapeDtypeStruct((nodes, feat), jnp.bfloat16),
            jax.ShapeDtypeStruct((feat, feat), jnp.float32),
        ],
        compiler_params=params(),
        cost_estimate=cost(6 * nodes * feat * feat, 30_000_000),
    )(in_rows, incoming, summed, initial, cotangent, weight)


def backward_kernel(part, nb, size, row_ref, col_ref, vals_ref, gmix_ref, out_ref, acc):
    step = pl.program_id(0)
    per_step = vals_ref.shape[0]

    @pl.when(step == 0)
    def _():
        def zero(j, _):
            acc[j] = jnp.zeros(acc.shape[1:], acc.dtype)
            return 0

        lax.fori_loop(0, acc.shape[0], zero, 0)

    for i in range(per_step):
        b = step * per_step + i
        col = col_ref[b]
        owner, inner = col // nb, lax.rem(col, nb)

        @pl.when(inner // size == part)
        def _():
            acc[owner * size + inner - part * size] += lax.dot_general(
                vals_ref[i],
                gmix_ref[row_ref[b]],
                (((0,), (0,)), ((), ())),
                preferred_element_type=jnp.float32,
            )

    @pl.when(step == pl.num_programs(0) - 1)
    def _():
        def write(j, _):
            out_ref[j] = (0.9 * acc[j]).astype(out_ref.dtype)
            return 0

        lax.fori_loop(0, acc.shape[0], write, 0)


def group_backward(part, parts, grp_row, grp_col, grp_vals, gmix, members):
    count, blk, _ = grp_vals.shape
    nb, _, feat = gmix.shape
    per_step = 16
    size = nb // parts
    shape = (members * size, blk, feat)
    return pl.pallas_call(
        lambda *refs: backward_kernel(part, nb, size, *refs),
        grid_spec=pltpu.PrefetchScalarGridSpec(
            num_scalar_prefetch=2,
            grid=(count // per_step,),
            in_specs=[
                pl.BlockSpec((per_step, blk, blk), lambda i, *_: (i, 0, 0)),
                full(gmix.shape),
            ],
            out_specs=full(shape),
            scratch_shapes=[pltpu.VMEM(shape, jnp.float32)],
        ),
        out_shape=jax.ShapeDtypeStruct(shape, jnp.bfloat16),
        compiler_params=params(),
        cost_estimate=cost(2 * count * blk * blk * feat // parts, 40_000_000 // parts),
    )(grp_row, grp_col, grp_vals, gmix)


def reduce_kernel(groups, members, scale, x_ref, out_ref, part, whole, done, sems):
    g, m = lax.axis_index("grp"), lax.axis_index("mem")
    rows = part.shape[1]
    barrier = pltpu.get_barrier_semaphore()
    mates = [lax.rem(m + k, members) for k in range(1, members)]
    peers = [lax.rem(g + k, groups) for k in range(1, groups)]
    for mate in mates:
        pl.semaphore_signal(barrier, inc=1, device_id=(g, mate), device_id_type=MESH)
    for peer in peers:
        pl.semaphore_signal(barrier, inc=1, device_id=(peer, m), device_id_type=MESH)
    pl.semaphore_wait(barrier, members + groups - 2)

    def at(index):
        return pl.ds(pl.multiple_of(index * rows, rows), rows)

    copies = []
    for k, mate in enumerate(mates):
        copies.append(
            pltpu.make_async_remote_copy(
                x_ref.at[at(mate)],
                part.at[m],
                sems.at[0, k],
                sems.at[1, k],
                device_id=(g, mate),
                device_id_type=MESH,
            )
        )
        copies[-1].start()
    part[m] = x_ref[at(m), :]
    for copy in copies:
        copy.wait()
    total = part[0]
    for k in range(1, members):
        total = total + part[k]
    whole[g] = total
    copies = []
    for k, peer in enumerate(peers):
        copies.append(
            pltpu.make_async_remote_copy(
                whole.at[g],
                whole.at[g],
                sems.at[2, k],
                sems.at[3, k],
                device_id=(peer, m),
                device_id_type=MESH,
            )
        )
        copies[-1].start()
    for copy in copies:
        copy.wait()
    total = whole[0]
    for k in range(1, groups):
        total = total + whole[k]
    done[m] = total * scale
    copies = []
    for k, mate in enumerate(mates):
        copies.append(
            pltpu.make_async_remote_copy(
                done.at[m],
                done.at[m],
                sems.at[4, k],
                sems.at[5, k],
                device_id=(g, mate),
                device_id_type=MESH,
            )
        )
        copies[-1].start()
    for copy in copies:
        copy.wait()
    for k in range(members):
        out_ref[k * rows : (k + 1) * rows, :] = done[k]


def all_reduce(x, scale, groups, members):
    rows, cols = x.shape
    share = rows // members
    return pl.pallas_call(
        lambda *refs: reduce_kernel(groups, members, scale, *refs),
        out_shape=jax.ShapeDtypeStruct(x.shape, x.dtype),
        in_specs=[pl.BlockSpec(memory_space=pltpu.VMEM)],
        out_specs=pl.BlockSpec(memory_space=pltpu.VMEM),
        scratch_shapes=[
            pltpu.VMEM((members, share, cols), jnp.float32),
            pltpu.VMEM((groups, share, cols), jnp.float32),
            pltpu.VMEM((members, share, cols), jnp.float32),
            pltpu.SemaphoreType.DMA((6, max(groups, members) - 1)),
        ],
        compiler_params=params(collective_id=0, has_side_effects=True),
        cost_estimate=cost(1_000_000, 4_000_000),
    )(x)


def per_device(
    hidden,
    initial,
    weight,
    grp_vals,
    grp_row,
    grp_col,
    bnd_vals,
    bnd_src,
    bnd_dst,
    bnd_row,
    cotangent,
):
    blk = grp_vals.shape[1]
    nodes, feat = hidden.shape
    nb = nodes // blk
    devices = lax.axis_size(AXES)
    groups, members = lax.axis_size("grp"), lax.axis_size("mem")
    count = bnd_vals.shape[0]
    blocks = hidden.reshape(nb, blk, feat)

    target = bnd_dst[:, 0]
    ids = jnp.arange(count, dtype=jnp.int32)
    place = jnp.sum(
        (target[:, None] == target[None, :]) & (ids[None, :] < ids[:, None]),
        axis=1,
        dtype=jnp.int32,
    )
    slot = target * 2 + place
    out_rows = jnp.max(
        jnp.where(
            slot[None, :] == jnp.arange(2 * devices, dtype=jnp.int32)[:, None],
            bnd_row[None, :],
            -1,
        ),
        axis=1,
    )
    in_rows = lax.all_to_all(
        out_rows.reshape(devices, 2), AXES, split_axis=0, concat_axis=0, tiled=True
    ).reshape(-1)
    table = lax.all_gather(blocks, "mem", axis=0, tiled=True)
    outgoing = partials(slot, bnd_src, bnd_vals, blocks, devices)
    outgoing, table, in_rows = lax.optimization_barrier((outgoing, table, in_rows))
    incoming = lax.all_to_all(
        outgoing.reshape(devices, 2 * blk, feat), AXES, split_axis=0, concat_axis=0, tiled=True
    )
    summed = group_forward(grp_row, grp_col, grp_vals, table, nb)
    output, gmix, local_weight = middle(
        in_rows, incoming, summed, initial, cotangent, weight, nodes * devices
    )
    gmix = gmix.reshape(nb, blk, feat)
    parts = 2
    tables = []
    for part in range(parts):
        term = group_backward(part, parts, grp_row, grp_col, grp_vals, gmix, members)
        tables.append(lax.psum_scatter(term, "mem", scatter_dimension=0, tiled=True))
    local_weight, term = lax.optimization_barrier((local_weight, term))
    grad_weight = all_reduce(local_weight, 0.5 / math.sqrt(nodes * devices), groups, members)
    return output, grad_weight, jnp.concatenate(tables, axis=0).reshape(nodes, feat)


def solution(mesh):
    return jax.shard_map(
        per_device,
        mesh=mesh,
        in_specs=(
            P(AXES, None),
            P(AXES, None),
            P(),
            P(AXES, None, None),
            P(AXES),
            P(AXES),
            P(AXES, None, None),
            P(AXES),
            P(AXES, None),
            P(AXES),
            P(AXES, None),
        ),
        out_specs=(P(AXES, None), P(), P(AXES, None)),
        check_vma=False,
    )
```

```python
import math

import jax
import jax.numpy as jnp
from jax import lax
from jax.experimental import pallas as pl
from jax.experimental.pallas import tpu as pltpu
from jax.sharding import PartitionSpec as P

AXES = ("grp", "mem")
MESH = pl.DeviceIdType.MESH
VMEM_LIMIT = 56 * 1024 * 1024
BATCH = 8


def params(**kw):
    return pltpu.CompilerParams(vmem_limit_bytes=VMEM_LIMIT, **kw)


def full(shape):
    return pl.BlockSpec(shape, lambda *_: (0,) * len(shape))


def cost(flops, moved):
    return pl.CostEstimate(flops=flops, bytes_accessed=moved, transcendentals=0)


def partial_kernel(slot_ref, src_ref, vals_ref, hid_ref, out_ref, stage, sem):
    step = pl.program_id(0)
    half = lax.rem(step, 2)
    per_step = vals_ref.shape[0]

    def drain(which):
        for i in range(per_step):
            pltpu.make_async_copy(stage.at[which, i], out_ref.at[0], sem.at[which, i]).wait()

    @pl.when(step >= 2)
    def _():
        drain(half)

    for i in range(per_step):
        edge = step * per_step + i
        stage[half, i] = jnp.dot(
            vals_ref[i], hid_ref[src_ref[edge]], preferred_element_type=jnp.float32
        ).astype(stage.dtype)
    for i in range(per_step):
        edge = step * per_step + i
        pltpu.make_async_copy(
            stage.at[half, i], out_ref.at[slot_ref[edge]], sem.at[half, i]
        ).start()

    @pl.when(step == pl.num_programs(0) - 1)
    def _():
        drain(1 - half)
        drain(half)


def partials(slot, bnd_src, bnd_vals, blocks, devices):
    count, blk, _ = bnd_vals.shape
    nb, _, feat = blocks.shape
    per_step = 16
    assert count % per_step == 0 and count >= 2 * per_step
    return pl.pallas_call(
        partial_kernel,
        grid_spec=pltpu.PrefetchScalarGridSpec(
            num_scalar_prefetch=2,
            grid=(count // per_step,),
            in_specs=[
                pl.BlockSpec((per_step, blk, blk), lambda i, *_: (i, 0, 0)),
                full(blocks.shape),
            ],
            out_specs=pl.BlockSpec(memory_space=pl.ANY),
            scratch_shapes=[
                pltpu.VMEM((2, per_step, blk, feat), jnp.bfloat16),
                pltpu.SemaphoreType.DMA((2, per_step)),
            ],
        ),
        out_shape=jax.ShapeDtypeStruct((devices * 2, blk, feat), jnp.bfloat16),
        compiler_params=params(),
        cost_estimate=cost(2 * count * blk * blk * feat, 3 * count * blk * feat),
    )(slot, bnd_src, bnd_vals, blocks)


def core_kernel(
    slot_order,
    slot_row,
    filled,
    grp_row,
    grp_col,
    edge_order,
    edge_row,
    edge_col,
    inc_hbm,
    table_hbm,
    vals_hbm,
    initial_hbm,
    cot_hbm,
    w_ref,
    out_hbm,
    term_hbm,
    gw_ref,
    ring,
    table,
    vals,
    initial,
    cot,
    acc,
    out,
    gmix,
    term,
    mixed_all,
    gpre_all,
    mw,
    ring_sem,
    table_sem,
    vals_sem,
    in_sem,
    out_sem,
    term_sem,
):
    nb, blk, feat = gmix.shape
    depth = ring_sem.shape[0] // BATCH
    chunks = vals_sem.shape[0]
    per_chunk = vals.shape[0] // chunks
    batches = (filled[0] + BATCH - 1) // BATCH

    def fetch(batch, i):
        at = lax.rem(batch, depth) * BATCH + i
        return pltpu.make_async_copy(
            inc_hbm.at[slot_order[batch * BATCH + i]], ring.at[at], ring_sem.at[at]
        )

    def fetch_batch(batch):
        @pl.when(batch < batches)
        def _():
            for i in range(BATCH):
                fetch(batch, i).start()

    for batch in range(depth):
        fetch_batch(batch)
    table_copy = pltpu.make_async_copy(table_hbm, table, table_sem)
    table_copy.start()

    def vals_copy(chunk):
        at = pl.ds(chunk * per_chunk, per_chunk)
        return pltpu.make_async_copy(vals_hbm.at[at], vals.at[at], vals_sem.at[chunk])

    def start_vals(chunk, _):
        vals_copy(chunk).start()
        return 0

    lax.fori_loop(0, chunks, start_vals, 0)
    initial_copy = pltpu.make_async_copy(initial_hbm, initial, in_sem.at[0])
    cot_copy = pltpu.make_async_copy(cot_hbm, cot, in_sem.at[1])
    initial_copy.start()
    cot_copy.start()

    def zero_acc(j, _):
        acc[j] = jnp.zeros(acc.shape[1:], acc.dtype)
        return 0

    def zero_term(j, _):
        term[j] = jnp.zeros(term.shape[1:], term.dtype)
        return 0

    lax.fori_loop(0, acc.shape[0], zero_acc, 0)
    lax.fori_loop(0, term.shape[0], zero_term, 0)
    eye = lax.broadcasted_iota(jnp.int32, (feat, feat), 0) == lax.broadcasted_iota(
        jnp.int32, (feat, feat), 1
    )
    mw[...] = (
        jnp.where(eye, 0.5, 0.0).astype(jnp.float32) + 0.5 * w_ref[...].astype(jnp.float32)
    ).astype(jnp.bfloat16)

    def add_batch(batch, _):
        for i in range(BATCH):
            fetch(batch, i).wait()
        for i in range(BATCH):
            at = lax.rem(batch, depth) * BATCH + i
            acc[slot_row[batch * BATCH + i]] += ring[at].astype(jnp.float32)
        fetch_batch(batch + depth)
        return 0

    lax.fori_loop(0, batches, add_batch, 0)
    table_copy.wait()

    def forward(chunk, _):
        vals_copy(chunk).wait()
        for i in range(per_chunk):
            b = chunk * per_chunk + i
            acc[grp_row[b]] += jnp.dot(
                vals[b], table[grp_col[b]], preferred_element_type=jnp.float32
            )
        return 0

    lax.fori_loop(0, chunks, forward, 0)
    initial_copy.wait()
    cot_copy.wait()
    wide = 4

    def dense(j, _):
        at = pl.ds(pl.multiple_of(j * wide * blk, wide * blk), wide * blk)
        summed = acc[pl.ds(j * wide, wide)].reshape(wide * blk, feat)
        mixed = (0.9 * summed + 0.1 * initial[at, :].astype(jnp.float32)).astype(jnp.bfloat16)
        pre = jnp.dot(mixed, mw[...], preferred_element_type=jnp.float32)
        sig = jax.nn.sigmoid(pre)
        out[at, :] = (pre * sig).astype(jnp.bfloat16)
        gpre = (cot[at, :].astype(jnp.float32) * sig * (1.0 + pre * (1.0 - sig))).astype(
            jnp.bfloat16
        )
        mixed_all[at, :] = mixed
        gpre_all[at, :] = gpre
        gmix[pl.ds(j * wide, wide)] = (
            lax.dot_general(
                gpre, mw[...], (((1,), (1,)), ((), ())), preferred_element_type=jnp.float32
            )
            .astype(jnp.bfloat16)
            .reshape(wide, blk, feat)
        )
        return 0

    lax.fori_loop(0, nb // wide, dense, 0)
    out_copy = pltpu.make_async_copy(out, out_hbm, out_sem)
    out_copy.start()
    gw_ref[...] = lax.dot_general(
        mixed_all[...], gpre_all[...], (((0,), (0,)), ((), ())), preferred_element_type=jnp.float32
    )

    def send_term(c, _):
        pltpu.make_async_copy(term.at[c], term_hbm.at[c], term_sem).start()
        return 0

    running = acc.at[0]
    running[...] = jnp.zeros((blk, feat), jnp.float32)

    def backward(chunk, sent):
        total = running[...]
        for i in range(per_chunk):
            b = chunk * per_chunk + i
            col = edge_col[b]
            same = (col == edge_col[jnp.maximum(b - 1, 0)]).astype(jnp.float32)
            total = total * same + lax.dot_general(
                vals[edge_order[b]],
                gmix[edge_row[b]],
                (((0,), (0,)), ((), ())),
                preferred_element_type=jnp.float32,
            )
            term[col] = (0.9 * total).astype(term.dtype)
        running[...] = total
        past = edge_col[chunk * per_chunk + per_chunk - 1]
        lax.fori_loop(sent, past, send_term, 0)
        return past

    sent = lax.fori_loop(0, chunks, backward, jnp.int32(0))
    lax.fori_loop(sent, term.shape[0], send_term, 0)
    out_copy.wait()
    pltpu.make_async_copy(term, term_hbm, term_sem).wait()


def core(scalars, incoming, table, grp_vals, initial, cotangent, weight, nb):
    count, blk, _ = grp_vals.shape
    nodes, feat = initial.shape
    ring, chunks = 4 * BATCH, 7
    assert count % chunks == 0 and incoming.shape[0] % BATCH == 0
    smem = pl.BlockSpec(memory_space=pltpu.SMEM)
    hbm = pl.BlockSpec(memory_space=pl.ANY)
    vmem = pl.BlockSpec(memory_space=pltpu.VMEM)
    bf16, dma = jnp.bfloat16, pltpu.SemaphoreType.DMA
    return pl.pallas_call(
        core_kernel,
        in_specs=[smem] * len(scalars) + [hbm] * 5 + [vmem],
        out_specs=[hbm, hbm, vmem],
        out_shape=[
            jax.ShapeDtypeStruct((nodes, feat), bf16),
            jax.ShapeDtypeStruct(table.shape, bf16),
            jax.ShapeDtypeStruct((feat, feat), jnp.float32),
        ],
        scratch_shapes=[
            pltpu.VMEM((ring, blk, feat), bf16),
            pltpu.VMEM(table.shape, bf16),
            pltpu.VMEM(grp_vals.shape, bf16),
            pltpu.VMEM((nodes, feat), bf16),
            pltpu.VMEM((nodes, feat), bf16),
            pltpu.VMEM((nb + 1, blk, feat), jnp.float32),
            pltpu.VMEM((nodes, feat), bf16),
            pltpu.VMEM((nb, blk, feat), bf16),
            pltpu.VMEM(table.shape, bf16),
            pltpu.VMEM((nodes, feat), bf16),
            pltpu.VMEM((nodes, feat), bf16),
            pltpu.VMEM((feat, feat), bf16),
            dma((ring,)),
            dma,
            dma((chunks,)),
            dma((2,)),
            dma,
            dma,
        ],
        compiler_params=params(),
        cost_estimate=cost(4 * count * blk * blk * feat + 6 * nodes * feat * feat, 60_000_000),
    )(*scalars, incoming, table, grp_vals, initial, cotangent, weight)


def reduce_kernel(groups, members, scale, x_ref, out_ref, part, whole, done, sems):
    g, m = lax.axis_index("grp"), lax.axis_index("mem")
    rows = part.shape[1]
    barrier = pltpu.get_barrier_semaphore()
    mates = [lax.rem(m + k, members) for k in range(1, members)]
    peers = [lax.rem(g + k, groups) for k in range(1, groups)]
    for mate in mates:
        pl.semaphore_signal(barrier, inc=1, device_id=(g, mate), device_id_type=MESH)
    for peer in peers:
        pl.semaphore_signal(barrier, inc=1, device_id=(peer, m), device_id_type=MESH)
    pl.semaphore_wait(barrier, members + groups - 2)

    def exchange(stage, targets, source, target):
        copies = []
        for k, (device, src) in enumerate(zip(targets, source)):
            copies.append(
                pltpu.make_async_remote_copy(
                    src,
                    target,
                    sems.at[2 * stage, k],
                    sems.at[2 * stage + 1, k],
                    device_id=device,
                    device_id_type=MESH,
                )
            )
            copies[-1].start()
        return copies

    def at(index):
        return pl.ds(pl.multiple_of(index * rows, rows), rows)

    def total(buffer):
        result = buffer[0]
        for k in range(1, buffer.shape[0]):
            result = result + buffer[k]
        return result

    far = [(peer, m) for peer in peers]
    copies = exchange(0, far, [x_ref.at[at(peer)] for peer in peers], part.at[g])
    part[g] = x_ref[at(g), :]
    for copy in copies:
        copy.wait()
    whole[m] = total(part)
    for copy in exchange(1, [(g, mate) for mate in mates], [whole.at[m]] * len(mates), whole.at[m]):
        copy.wait()
    done[g] = total(whole) * scale
    for copy in exchange(2, far, [done.at[g]] * len(far), done.at[g]):
        copy.wait()
    for k in range(groups):
        out_ref[k * rows : (k + 1) * rows, :] = done[k]


def all_reduce(x, scale, groups, members):
    rows, cols = x.shape
    share = rows // groups
    return pl.pallas_call(
        lambda *refs: reduce_kernel(groups, members, scale, *refs),
        out_shape=jax.ShapeDtypeStruct(x.shape, x.dtype),
        in_specs=[pl.BlockSpec(memory_space=pltpu.VMEM)],
        out_specs=pl.BlockSpec(memory_space=pltpu.VMEM),
        scratch_shapes=[
            pltpu.VMEM((groups, share, cols), jnp.float32),
            pltpu.VMEM((members, share, cols), jnp.float32),
            pltpu.VMEM((groups, share, cols), jnp.float32),
            pltpu.SemaphoreType.DMA((6, max(groups, members) - 1)),
        ],
        compiler_params=params(collective_id=0, has_side_effects=True),
        cost_estimate=cost(1_000_000, 4_000_000),
    )(x)


def sorted_by(key, *values):
    ids = jnp.arange(key.shape[0], dtype=jnp.int32)
    ahead = (key[None, :] < key[:, None]) | (
        (key[None, :] == key[:, None]) & (ids[None, :] < ids[:, None])
    )
    rank = jnp.sum(ahead, axis=1, dtype=jnp.int32)
    hit = rank[None, :] == ids[:, None]
    return [jnp.sum(jnp.where(hit, value[None, :], 0), axis=1) for value in (ids, *values)]


def per_device(
    hidden,
    initial,
    weight,
    grp_vals,
    grp_row,
    grp_col,
    bnd_vals,
    bnd_src,
    bnd_dst,
    bnd_row,
    cotangent,
):
    blk = grp_vals.shape[1]
    nodes, feat = hidden.shape
    nb = nodes // blk
    devices = lax.axis_size(AXES)
    groups, members = lax.axis_size("grp"), lax.axis_size("mem")
    count = bnd_vals.shape[0]
    blocks = hidden.reshape(nb, blk, feat)

    target = bnd_dst[:, 0]
    ids = jnp.arange(count, dtype=jnp.int32)
    place = jnp.sum(
        (target[:, None] == target[None, :]) & (ids[None, :] < ids[:, None]),
        axis=1,
        dtype=jnp.int32,
    )
    slot = target * 2 + place
    out_rows = jnp.max(
        jnp.where(
            slot[None, :] == jnp.arange(2 * devices, dtype=jnp.int32)[:, None],
            bnd_row[None, :],
            -1,
        ),
        axis=1,
    )
    in_rows = lax.all_to_all(
        out_rows.reshape(devices, 2), AXES, split_axis=0, concat_axis=0, tiled=True
    ).reshape(-1)
    table = lax.all_gather(blocks, "mem", axis=0, tiled=True)
    outgoing = partials(slot, bnd_src, bnd_vals, blocks, devices)
    outgoing, grp_row, grp_col = lax.optimization_barrier((outgoing, grp_row, grp_col))
    incoming = lax.all_to_all(
        outgoing.reshape(devices, 2 * blk, feat), AXES, split_axis=0, concat_axis=0, tiled=True
    )
    edge_order, edge_row, edge_col = sorted_by(grp_col, grp_row, grp_col)
    empty = in_rows < 0
    slot_order, slot_row = sorted_by(
        empty.astype(jnp.int32), jnp.where(empty, nb, in_rows)
    )
    filled = jnp.sum(~empty, dtype=jnp.int32)[None]
    output, term, local_weight = core(
        (slot_order, slot_row, filled, grp_row, grp_col, edge_order, edge_row, edge_col),
        incoming.reshape(2 * devices, blk, feat),
        table,
        grp_vals,
        initial,
        cotangent,
        weight,
        nb,
    )
    grad_hidden = lax.psum_scatter(term, "mem", scatter_dimension=0, tiled=True)
    grad_weight = all_reduce(local_weight, 0.5 / math.sqrt(nodes * devices), groups, members)
    return output, grad_weight, grad_hidden.reshape(nodes, feat)


def solution(mesh):
    return jax.shard_map(
        per_device,
        mesh=mesh,
        in_specs=(
            P(AXES, None),
            P(AXES, None),
            P(),
            P(AXES, None, None),
            P(AXES),
            P(AXES),
            P(AXES, None, None),
            P(AXES),
            P(AXES, None),
            P(AXES),
            P(AXES, None),
        ),
        out_specs=(P(AXES, None), P(), P(AXES, None)),
        check_vma=False,
    )
```

```python
import math

import jax
import jax.numpy as jnp
from jax import lax
from jax.experimental import pallas as pl
from jax.experimental.pallas import tpu as pltpu
from jax.sharding import PartitionSpec as P

AXES = ("grp", "mem")
MESH = pl.DeviceIdType.MESH
VMEM_LIMIT = 56 * 1024 * 1024
BATCH = 8


def params(**kw):
    return pltpu.CompilerParams(vmem_limit_bytes=VMEM_LIMIT, **kw)


def full(shape):
    return pl.BlockSpec(shape, lambda *_: (0,) * len(shape))


def cost(flops, moved):
    return pl.CostEstimate(flops=flops, bytes_accessed=moved, transcendentals=0)


def partial_kernel(slot_ref, src_ref, vals_ref, hid_ref, out_ref, stage, sem):
    step = pl.program_id(0)
    half = lax.rem(step, 2)
    per_step = vals_ref.shape[0]

    def drain(which):
        for i in range(per_step):
            pltpu.make_async_copy(stage.at[which, i], out_ref.at[0], sem.at[which, i]).wait()

    @pl.when(step >= 2)
    def _():
        drain(half)

    for i in range(per_step):
        edge = step * per_step + i
        stage[half, i] = jnp.dot(
            vals_ref[i], hid_ref[src_ref[edge]], preferred_element_type=jnp.float32
        ).astype(stage.dtype)
    for i in range(per_step):
        edge = step * per_step + i
        pltpu.make_async_copy(
            stage.at[half, i], out_ref.at[slot_ref[edge]], sem.at[half, i]
        ).start()

    @pl.when(step == pl.num_programs(0) - 1)
    def _():
        drain(1 - half)
        drain(half)


def partials(slot, bnd_src, bnd_vals, blocks, devices):
    count, blk, _ = bnd_vals.shape
    nb, _, feat = blocks.shape
    per_step = 16
    assert count % per_step == 0 and count >= 2 * per_step
    return pl.pallas_call(
        partial_kernel,
        grid_spec=pltpu.PrefetchScalarGridSpec(
            num_scalar_prefetch=2,
            grid=(count // per_step,),
            in_specs=[
                pl.BlockSpec((per_step, blk, blk), lambda i, *_: (i, 0, 0)),
                full(blocks.shape),
            ],
            out_specs=pl.BlockSpec(memory_space=pl.ANY),
            scratch_shapes=[
                pltpu.VMEM((2, per_step, blk, feat), jnp.bfloat16),
                pltpu.SemaphoreType.DMA((2, per_step)),
            ],
        ),
        out_shape=jax.ShapeDtypeStruct((devices * 2, blk, feat), jnp.bfloat16),
        compiler_params=params(),
        cost_estimate=cost(2 * count * blk * blk * feat, 3 * count * blk * feat),
    )(slot, bnd_src, bnd_vals, blocks)


def core_kernel(
    slot_order,
    slot_row,
    filled,
    grp_row,
    grp_col,
    edge_order,
    edge_row,
    edge_col,
    inc_hbm,
    table_hbm,
    vals_hbm,
    initial_hbm,
    cot_hbm,
    w_ref,
    out_hbm,
    term_hbm,
    gw_ref,
    ring,
    table,
    vals,
    initial,
    cot,
    acc,
    out,
    gmix,
    term,
    mixed_all,
    gpre_all,
    mw,
    ring_sem,
    table_sem,
    vals_sem,
    in_sem,
    out_sem,
    term_sem,
):
    nb, blk, feat = gmix.shape
    depth = ring_sem.shape[0] // BATCH
    chunks = vals_sem.shape[0]
    per_chunk = vals.shape[0] // chunks
    batches = (filled[0] + BATCH - 1) // BATCH

    def fetch(batch, i):
        at = lax.rem(batch, depth) * BATCH + i
        return pltpu.make_async_copy(
            inc_hbm.at[slot_order[batch * BATCH + i]], ring.at[at], ring_sem.at[at]
        )

    def fetch_batch(batch):
        @pl.when(batch < batches)
        def _():
            for i in range(BATCH):
                fetch(batch, i).start()

    for batch in range(depth):
        fetch_batch(batch)
    table_copy = pltpu.make_async_copy(table_hbm, table, table_sem)
    table_copy.start()

    def vals_copy(chunk):
        at = pl.ds(chunk * per_chunk, per_chunk)
        return pltpu.make_async_copy(vals_hbm.at[at], vals.at[at], vals_sem.at[chunk])

    def start_vals(chunk, _):
        vals_copy(chunk).start()
        return 0

    lax.fori_loop(0, chunks, start_vals, 0)
    initial_copy = pltpu.make_async_copy(initial_hbm, initial, in_sem.at[0])
    cot_copy = pltpu.make_async_copy(cot_hbm, cot, in_sem.at[1])
    initial_copy.start()
    cot_copy.start()

    def zero_acc(j, _):
        acc[j] = jnp.zeros(acc.shape[1:], acc.dtype)
        return 0

    def zero_term(j, _):
        term[j] = jnp.zeros(term.shape[1:], term.dtype)
        return 0

    lax.fori_loop(0, acc.shape[0], zero_acc, 0)
    lax.fori_loop(0, term.shape[0], zero_term, 0)
    eye = lax.broadcasted_iota(jnp.int32, (feat, feat), 0) == lax.broadcasted_iota(
        jnp.int32, (feat, feat), 1
    )
    mw[...] = (
        jnp.where(eye, 0.5, 0.0).astype(jnp.float32) + 0.5 * w_ref[...].astype(jnp.float32)
    ).astype(jnp.bfloat16)

    def add_batch(batch, _):
        for i in range(BATCH):
            fetch(batch, i).wait()
        for i in range(BATCH):
            at = lax.rem(batch, depth) * BATCH + i
            acc[slot_row[batch * BATCH + i]] += ring[at].astype(jnp.float32)
        fetch_batch(batch + depth)
        return 0

    lax.fori_loop(0, batches, add_batch, 0)
    table_copy.wait()

    def forward(chunk, _):
        vals_copy(chunk).wait()
        for i in range(per_chunk):
            b = chunk * per_chunk + i
            acc[grp_row[b]] += jnp.dot(
                vals[b], table[grp_col[b]], preferred_element_type=jnp.float32
            )
        return 0

    lax.fori_loop(0, chunks, forward, 0)
    initial_copy.wait()
    cot_copy.wait()
    wide = 4

    def dense(j, _):
        at = pl.ds(pl.multiple_of(j * wide * blk, wide * blk), wide * blk)
        summed = acc[pl.ds(j * wide, wide)].reshape(wide * blk, feat)
        mixed = (0.9 * summed + 0.1 * initial[at, :].astype(jnp.float32)).astype(jnp.bfloat16)
        pre = jnp.dot(mixed, mw[...], preferred_element_type=jnp.float32)
        sig = jax.nn.sigmoid(pre)
        out[at, :] = (pre * sig).astype(jnp.bfloat16)
        gpre = (cot[at, :].astype(jnp.float32) * sig * (1.0 + pre * (1.0 - sig))).astype(
            jnp.bfloat16
        )
        mixed_all[at, :] = mixed
        gpre_all[at, :] = gpre
        gmix[pl.ds(j * wide, wide)] = (
            lax.dot_general(
                gpre, mw[...], (((1,), (1,)), ((), ())), preferred_element_type=jnp.float32
            )
            .astype(jnp.bfloat16)
            .reshape(wide, blk, feat)
        )
        return 0

    lax.fori_loop(0, nb // wide, dense, 0)
    out_copy = pltpu.make_async_copy(out, out_hbm, out_sem)
    out_copy.start()
    gw_ref[...] = lax.dot_general(
        mixed_all[...], gpre_all[...], (((0,), (0,)), ((), ())), preferred_element_type=jnp.float32
    )

    def send_term(c, _):
        pltpu.make_async_copy(term.at[c], term_hbm.at[c], term_sem).start()
        return 0

    running = acc.at[0]
    running[...] = jnp.zeros((blk, feat), jnp.float32)

    def backward(chunk, sent):
        total = running[...]
        for i in range(per_chunk):
            b = chunk * per_chunk + i
            col = edge_col[b]
            same = (col == edge_col[jnp.maximum(b - 1, 0)]).astype(jnp.float32)
            total = total * same + lax.dot_general(
                vals[edge_order[b]],
                gmix[edge_row[b]],
                (((0,), (0,)), ((), ())),
                preferred_element_type=jnp.float32,
            )
            term[col] = (0.9 * total).astype(term.dtype)
        running[...] = total
        past = edge_col[chunk * per_chunk + per_chunk - 1]
        lax.fori_loop(sent, past, send_term, 0)
        return past

    sent = lax.fori_loop(0, chunks, backward, jnp.int32(0))
    lax.fori_loop(sent, term.shape[0], send_term, 0)
    out_copy.wait()
    pltpu.make_async_copy(term, term_hbm, term_sem).wait()


def core(scalars, incoming, table, grp_vals, initial, cotangent, weight, nb):
    count, blk, _ = grp_vals.shape
    nodes, feat = initial.shape
    ring, chunks = 4 * BATCH, 7
    assert count % chunks == 0 and incoming.shape[0] % BATCH == 0
    smem = pl.BlockSpec(memory_space=pltpu.SMEM)
    hbm = pl.BlockSpec(memory_space=pl.ANY)
    vmem = pl.BlockSpec(memory_space=pltpu.VMEM)
    bf16, dma = jnp.bfloat16, pltpu.SemaphoreType.DMA
    return pl.pallas_call(
        core_kernel,
        in_specs=[smem] * len(scalars) + [hbm] * 5 + [vmem],
        out_specs=[hbm, hbm, vmem],
        out_shape=[
            jax.ShapeDtypeStruct((nodes, feat), bf16),
            jax.ShapeDtypeStruct(table.shape, bf16),
            jax.ShapeDtypeStruct((feat, feat), jnp.float32),
        ],
        scratch_shapes=[
            pltpu.VMEM((ring, blk, feat), bf16),
            pltpu.VMEM(table.shape, bf16),
            pltpu.VMEM(grp_vals.shape, bf16),
            pltpu.VMEM((nodes, feat), bf16),
            pltpu.VMEM((nodes, feat), bf16),
            pltpu.VMEM((nb + 1, blk, feat), jnp.float32),
            pltpu.VMEM((nodes, feat), bf16),
            pltpu.VMEM((nb, blk, feat), bf16),
            pltpu.VMEM(table.shape, bf16),
            pltpu.VMEM((nodes, feat), bf16),
            pltpu.VMEM((nodes, feat), bf16),
            pltpu.VMEM((feat, feat), bf16),
            dma((ring,)),
            dma,
            dma((chunks,)),
            dma((2,)),
            dma,
            dma,
        ],
        compiler_params=params(),
        cost_estimate=cost(4 * count * blk * blk * feat + 6 * nodes * feat * feat, 60_000_000),
    )(*scalars, incoming, table, grp_vals, initial, cotangent, weight)


def reduce_kernel(groups, members, scale, x_ref, out_ref, part, whole, done, sems):
    g, m = lax.axis_index("grp"), lax.axis_index("mem")
    rows = part.shape[1]
    barrier = pltpu.get_barrier_semaphore()
    mates = [lax.rem(m + k, members) for k in range(1, members)]
    peers = [lax.rem(g + k, groups) for k in range(1, groups)]
    for mate in mates:
        pl.semaphore_signal(barrier, inc=1, device_id=(g, mate), device_id_type=MESH)
    for peer in peers:
        pl.semaphore_signal(barrier, inc=1, device_id=(peer, m), device_id_type=MESH)
    pl.semaphore_wait(barrier, members + groups - 2)

    def exchange(stage, targets, source, target):
        copies = []
        for k, (device, src) in enumerate(zip(targets, source)):
            copies.append(
                pltpu.make_async_remote_copy(
                    src,
                    target,
                    sems.at[2 * stage, k],
                    sems.at[2 * stage + 1, k],
                    device_id=device,
                    device_id_type=MESH,
                )
            )
            copies[-1].start()
        return copies

    def at(index):
        return pl.ds(pl.multiple_of(index * rows, rows), rows)

    def total(buffer):
        result = buffer[0]
        for k in range(1, buffer.shape[0]):
            result = result + buffer[k]
        return result

    far = [(peer, m) for peer in peers]
    copies = exchange(0, far, [x_ref.at[at(peer)] for peer in peers], part.at[g])
    part[g] = x_ref[at(g), :]
    for copy in copies:
        copy.wait()
    whole[m] = total(part)
    for copy in exchange(1, [(g, mate) for mate in mates], [whole.at[m]] * len(mates), whole.at[m]):
        copy.wait()
    done[g] = total(whole) * scale
    for copy in exchange(2, far, [done.at[g]] * len(far), done.at[g]):
        copy.wait()
    for k in range(groups):
        out_ref[k * rows : (k + 1) * rows, :] = done[k]


def all_reduce(x, scale, groups, members):
    rows, cols = x.shape
    share = rows // groups
    return pl.pallas_call(
        lambda *refs: reduce_kernel(groups, members, scale, *refs),
        out_shape=jax.ShapeDtypeStruct(x.shape, x.dtype),
        in_specs=[pl.BlockSpec(memory_space=pltpu.VMEM)],
        out_specs=pl.BlockSpec(memory_space=pltpu.VMEM),
        scratch_shapes=[
            pltpu.VMEM((groups, share, cols), jnp.float32),
            pltpu.VMEM((members, share, cols), jnp.float32),
            pltpu.VMEM((groups, share, cols), jnp.float32),
            pltpu.SemaphoreType.DMA((6, max(groups, members) - 1)),
        ],
        compiler_params=params(collective_id=0, has_side_effects=True),
        cost_estimate=cost(1_000_000, 4_000_000),
    )(x)


def sorted_by(key, *values):
    ids = jnp.arange(key.shape[0], dtype=jnp.int32)
    ahead = (key[None, :] < key[:, None]) | (
        (key[None, :] == key[:, None]) & (ids[None, :] < ids[:, None])
    )
    rank = jnp.sum(ahead, axis=1, dtype=jnp.int32)
    hit = rank[None, :] == ids[:, None]
    return [jnp.sum(jnp.where(hit, value[None, :], 0), axis=1) for value in (ids, *values)]


def per_device(
    hidden,
    initial,
    weight,
    grp_vals,
    grp_row,
    grp_col,
    bnd_vals,
    bnd_src,
    bnd_dst,
    bnd_row,
    cotangent,
):
    blk = grp_vals.shape[1]
    nodes, feat = hidden.shape
    nb = nodes // blk
    devices = lax.axis_size(AXES)
    groups, members = lax.axis_size("grp"), lax.axis_size("mem")
    count = bnd_vals.shape[0]
    blocks = hidden.reshape(nb, blk, feat)

    target = bnd_dst[:, 0]
    ids = jnp.arange(count, dtype=jnp.int32)
    place = jnp.sum(
        (target[:, None] == target[None, :]) & (ids[None, :] < ids[:, None]),
        axis=1,
        dtype=jnp.int32,
    )
    slot = target * 2 + place
    out_rows = jnp.max(
        jnp.where(
            slot[None, :] == jnp.arange(2 * devices, dtype=jnp.int32)[:, None],
            bnd_row[None, :],
            -1,
        ),
        axis=1,
    )
    in_rows = lax.all_to_all(
        out_rows.reshape(devices, 2), AXES, split_axis=0, concat_axis=0, tiled=True
    ).reshape(-1)
    table = lax.all_gather(blocks, "mem", axis=0, tiled=True)
    outgoing = partials(slot, bnd_src, bnd_vals, blocks, devices)
    edge_order, edge_row, edge_col = sorted_by(grp_col, grp_row, grp_col)
    empty = in_rows < 0
    slot_order, slot_row = sorted_by(
        empty.astype(jnp.int32), jnp.where(empty, nb, in_rows)
    )
    filled = jnp.sum(~empty, dtype=jnp.int32)[None]
    scalars = (slot_order, slot_row, filled, grp_row, grp_col, edge_order, edge_row, edge_col)
    outgoing, table, scalars = lax.optimization_barrier((outgoing, table, scalars))
    incoming = lax.all_to_all(
        outgoing.reshape(devices, 2 * blk, feat), AXES, split_axis=0, concat_axis=0, tiled=True
    )
    output, term, local_weight = core(
        scalars,
        incoming.reshape(2 * devices, blk, feat),
        table,
        grp_vals,
        initial,
        cotangent,
        weight,
        nb,
    )
    grad_hidden = lax.psum_scatter(term, "mem", scatter_dimension=0, tiled=True)
    grad_weight = all_reduce(local_weight, 0.5 / math.sqrt(nodes * devices), groups, members)
    return output, grad_weight, grad_hidden.reshape(nodes, feat)


def solution(mesh):
    return jax.shard_map(
        per_device,
        mesh=mesh,
        in_specs=(
            P(AXES, None),
            P(AXES, None),
            P(),
            P(AXES, None, None),
            P(AXES),
            P(AXES),
            P(AXES, None, None),
            P(AXES),
            P(AXES, None),
            P(AXES),
            P(AXES, None),
        ),
        out_specs=(P(AXES, None), P(), P(AXES, None)),
        check_vma=False,
    )
```

```python
import math

import jax
import jax.numpy as jnp
from jax import lax
from jax.experimental import pallas as pl
from jax.experimental.pallas import tpu as pltpu
from jax.sharding import PartitionSpec as P

AXES = ("grp", "mem")
MESH = pl.DeviceIdType.MESH
VMEM_LIMIT = 56 * 1024 * 1024
BATCH = 8


def params(**kw):
    return pltpu.CompilerParams(vmem_limit_bytes=VMEM_LIMIT, **kw)


def full(shape):
    return pl.BlockSpec(shape, lambda *_: (0,) * len(shape))


def cost(flops, moved):
    return pl.CostEstimate(flops=flops, bytes_accessed=moved, transcendentals=0)


def partial_kernel(slot_ref, src_ref, vals_ref, hid_ref, out_ref, stage, sem):
    step = pl.program_id(0)
    half = lax.rem(step, 2)
    per_step = vals_ref.shape[0]

    def drain(which):
        for i in range(per_step):
            pltpu.make_async_copy(stage.at[which, i], out_ref.at[0], sem.at[which, i]).wait()

    @pl.when(step >= 2)
    def _():
        drain(half)

    for i in range(per_step):
        edge = step * per_step + i
        stage[half, i] = jnp.dot(
            vals_ref[i], hid_ref[src_ref[edge]], preferred_element_type=jnp.float32
        ).astype(stage.dtype)
    for i in range(per_step):
        edge = step * per_step + i
        pltpu.make_async_copy(
            stage.at[half, i], out_ref.at[slot_ref[edge]], sem.at[half, i]
        ).start()

    @pl.when(step == pl.num_programs(0) - 1)
    def _():
        drain(1 - half)
        drain(half)


def partials(slot, bnd_src, bnd_vals, blocks, devices):
    count, blk, _ = bnd_vals.shape
    nb, _, feat = blocks.shape
    per_step = 16
    assert count % per_step == 0 and count >= 2 * per_step
    return pl.pallas_call(
        partial_kernel,
        grid_spec=pltpu.PrefetchScalarGridSpec(
            num_scalar_prefetch=2,
            grid=(count // per_step,),
            in_specs=[
                pl.BlockSpec((per_step, blk, blk), lambda i, *_: (i, 0, 0)),
                full(blocks.shape),
            ],
            out_specs=pl.BlockSpec(memory_space=pl.ANY),
            scratch_shapes=[
                pltpu.VMEM((2, per_step, blk, feat), jnp.bfloat16),
                pltpu.SemaphoreType.DMA((2, per_step)),
            ],
        ),
        out_shape=jax.ShapeDtypeStruct((devices * 2, blk, feat), jnp.bfloat16),
        compiler_params=params(),
        cost_estimate=cost(2 * count * blk * blk * feat, 3 * count * blk * feat),
    )(slot, bnd_src, bnd_vals, blocks)


def core_kernel(
    slot_order,
    slot_row,
    filled,
    grp_row,
    grp_col,
    edge_order,
    edge_row,
    edge_col,
    inc_hbm,
    table_hbm,
    vals_hbm,
    initial_hbm,
    cot_hbm,
    w_ref,
    out_hbm,
    term_hbm,
    gw_ref,
    ring,
    table,
    vals,
    initial,
    cot,
    acc,
    running,
    out,
    gmix,
    term,
    mixed_all,
    gpre_all,
    mw,
    ring_sem,
    table_sem,
    vals_sem,
    in_sem,
    out_sem,
    term_sem,
):
    nb, blk, feat = gmix.shape
    depth = ring_sem.shape[0] // BATCH
    chunks = vals_sem.shape[0]
    per_chunk = vals.shape[0] // chunks
    batches = (filled[0] + BATCH - 1) // BATCH

    def fetch(batch, i):
        at = lax.rem(batch, depth) * BATCH + i
        return pltpu.make_async_copy(
            inc_hbm.at[slot_order[batch * BATCH + i]], ring.at[at], ring_sem.at[at]
        )

    def fetch_batch(batch):
        @pl.when(batch < batches)
        def _():
            for i in range(BATCH):
                fetch(batch, i).start()

    for batch in range(depth):
        fetch_batch(batch)
    table_copy = pltpu.make_async_copy(table_hbm, table, table_sem)
    table_copy.start()

    def vals_copy(chunk):
        at = pl.ds(chunk * per_chunk, per_chunk)
        return pltpu.make_async_copy(vals_hbm.at[at], vals.at[at], vals_sem.at[chunk])

    def start_vals(chunk, _):
        vals_copy(chunk).start()
        return 0

    lax.fori_loop(0, chunks, start_vals, 0)
    initial_copy = pltpu.make_async_copy(initial_hbm, initial, in_sem.at[0])
    cot_copy = pltpu.make_async_copy(cot_hbm, cot, in_sem.at[1])
    initial_copy.start()
    cot_copy.start()

    def zero_acc(j, _):
        acc[j] = jnp.zeros(acc.shape[1:], acc.dtype)
        return 0

    def zero_term(j, _):
        term[j] = jnp.zeros(term.shape[1:], term.dtype)
        return 0

    lax.fori_loop(0, nb, zero_acc, 0)
    lax.fori_loop(0, term.shape[0], zero_term, 0)
    eye = lax.broadcasted_iota(jnp.int32, (feat, feat), 0) == lax.broadcasted_iota(
        jnp.int32, (feat, feat), 1
    )
    mw[...] = (
        jnp.where(eye, 0.5, 0.0).astype(jnp.float32) + 0.5 * w_ref[...].astype(jnp.float32)
    ).astype(jnp.bfloat16)

    def follows(key, at):
        return (key[at] == key[jnp.maximum(at - 1, 0)]).astype(jnp.float32)

    def add_batch(batch, _):
        for i in range(BATCH):
            fetch(batch, i).wait()
        total = running[...]
        for i in range(BATCH):
            at = batch * BATCH + i
            total = total * follows(slot_row, at) + ring[
                lax.rem(batch, depth) * BATCH + i
            ].astype(jnp.float32)
            acc[slot_row[at]] = total
        running[...] = total
        fetch_batch(batch + depth)
        return 0

    running[...] = jnp.zeros_like(running)
    lax.fori_loop(0, batches, add_batch, 0)
    table_copy.wait()

    def forward(chunk, _):
        vals_copy(chunk).wait()
        for i in range(per_chunk):
            b = chunk * per_chunk + i
            acc[grp_row[b]] += jnp.dot(
                vals[b], table[grp_col[b]], preferred_element_type=jnp.float32
            )
        return 0

    lax.fori_loop(0, chunks, forward, 0)
    initial_copy.wait()
    cot_copy.wait()
    wide = 4

    def dense(j, _):
        at = pl.ds(pl.multiple_of(j * wide * blk, wide * blk), wide * blk)
        summed = acc[pl.ds(j * wide, wide)].reshape(wide * blk, feat)
        mixed = (0.9 * summed + 0.1 * initial[at, :].astype(jnp.float32)).astype(jnp.bfloat16)
        pre = jnp.dot(mixed, mw[...], preferred_element_type=jnp.float32)
        sig = jax.nn.sigmoid(pre)
        out[at, :] = (pre * sig).astype(jnp.bfloat16)
        gpre = (cot[at, :].astype(jnp.float32) * sig * (1.0 + pre * (1.0 - sig))).astype(
            jnp.bfloat16
        )
        mixed_all[at, :] = mixed
        gpre_all[at, :] = gpre
        gmix[pl.ds(j * wide, wide)] = (
            lax.dot_general(
                gpre, mw[...], (((1,), (1,)), ((), ())), preferred_element_type=jnp.float32
            )
            .astype(jnp.bfloat16)
            .reshape(wide, blk, feat)
        )
        return 0

    lax.fori_loop(0, nb // wide, dense, 0)
    out_copy = pltpu.make_async_copy(out, out_hbm, out_sem)
    out_copy.start()
    gw_ref[...] = lax.dot_general(
        mixed_all[...], gpre_all[...], (((0,), (0,)), ((), ())), preferred_element_type=jnp.float32
    )

    def send_term(c, _):
        pltpu.make_async_copy(term.at[c], term_hbm.at[c], term_sem).start()
        return 0

    running[...] = jnp.zeros_like(running)

    def backward(chunk, sent):
        total = running[...]
        for i in range(per_chunk):
            b = chunk * per_chunk + i
            col = edge_col[b]
            total = total * follows(edge_col, b) + lax.dot_general(
                vals[edge_order[b]],
                gmix[edge_row[b]],
                (((0,), (0,)), ((), ())),
                preferred_element_type=jnp.float32,
            )
            term[col] = (0.9 * total).astype(term.dtype)
        running[...] = total
        past = edge_col[chunk * per_chunk + per_chunk - 1]
        lax.fori_loop(sent, past, send_term, 0)
        return past

    sent = lax.fori_loop(0, chunks, backward, jnp.int32(0))
    lax.fori_loop(sent, term.shape[0], send_term, 0)
    out_copy.wait()
    pltpu.make_async_copy(term, term_hbm, term_sem).wait()


def core(scalars, incoming, table, grp_vals, initial, cotangent, weight, nb):
    count, blk, _ = grp_vals.shape
    nodes, feat = initial.shape
    ring, chunks = 16 * BATCH, 7
    assert count % chunks == 0 and incoming.shape[0] % BATCH == 0
    smem = pl.BlockSpec(memory_space=pltpu.SMEM)
    hbm = pl.BlockSpec(memory_space=pl.ANY)
    vmem = pl.BlockSpec(memory_space=pltpu.VMEM)
    bf16, dma = jnp.bfloat16, pltpu.SemaphoreType.DMA
    return pl.pallas_call(
        core_kernel,
        in_specs=[smem] * len(scalars) + [hbm] * 5 + [vmem],
        out_specs=[hbm, hbm, vmem],
        out_shape=[
            jax.ShapeDtypeStruct((nodes, feat), bf16),
            jax.ShapeDtypeStruct(table.shape, bf16),
            jax.ShapeDtypeStruct((feat, feat), jnp.float32),
        ],
        scratch_shapes=[
            pltpu.VMEM((ring, blk, feat), bf16),
            pltpu.VMEM(table.shape, bf16),
            pltpu.VMEM(grp_vals.shape, bf16),
            pltpu.VMEM((nodes, feat), bf16),
            pltpu.VMEM((nodes, feat), bf16),
            pltpu.VMEM((nb + 1, blk, feat), jnp.float32),
            pltpu.VMEM((blk, feat), jnp.float32),
            pltpu.VMEM((nodes, feat), bf16),
            pltpu.VMEM((nb, blk, feat), bf16),
            pltpu.VMEM(table.shape, bf16),
            pltpu.VMEM((nodes, feat), bf16),
            pltpu.VMEM((nodes, feat), bf16),
            pltpu.VMEM((feat, feat), bf16),
            dma((ring,)),
            dma,
            dma((chunks,)),
            dma((2,)),
            dma,
            dma,
        ],
        compiler_params=params(),
        cost_estimate=cost(4 * count * blk * blk * feat + 6 * nodes * feat * feat, 60_000_000),
    )(*scalars, incoming, table, grp_vals, initial, cotangent, weight)


def reduce_kernel(groups, members, x_ref, out_ref, part, whole, done, sems):
    g, m = lax.axis_index("grp"), lax.axis_index("mem")
    rows = part.shape[1]
    barrier = pltpu.get_barrier_semaphore()
    mates = [lax.rem(m + k, members) for k in range(1, members)]
    peers = [lax.rem(g + k, groups) for k in range(1, groups)]
    for mate in mates:
        pl.semaphore_signal(barrier, inc=1, device_id=(g, mate), device_id_type=MESH)
    for peer in peers:
        pl.semaphore_signal(barrier, inc=1, device_id=(peer, m), device_id_type=MESH)
    pl.semaphore_wait(barrier, members + groups - 2)

    def exchange(stage, targets, source, target):
        copies = []
        for k, (device, src) in enumerate(zip(targets, source)):
            copies.append(
                pltpu.make_async_remote_copy(
                    src,
                    target,
                    sems.at[2 * stage, k],
                    sems.at[2 * stage + 1, k],
                    device_id=device,
                    device_id_type=MESH,
                )
            )
            copies[-1].start()
        return copies

    def at(index):
        return pl.ds(pl.multiple_of(index * rows, rows), rows)

    def total(buffer):
        result = buffer[0]
        for k in range(1, buffer.shape[0]):
            result = result + buffer[k]
        return result

    far = [(peer, m) for peer in peers]
    copies = exchange(0, far, [x_ref.at[at(peer)] for peer in peers], part.at[g])
    part[g] = x_ref[at(g), :]
    for copy in copies:
        copy.wait()
    whole[m] = total(part)
    for copy in exchange(1, [(g, mate) for mate in mates], [whole.at[m]] * len(mates), whole.at[m]):
        copy.wait()
    done[g] = total(whole)
    for copy in exchange(2, far, [done.at[g]] * len(far), done.at[g]):
        copy.wait()
    for k in range(groups):
        out_ref[k * rows : (k + 1) * rows, :] = done[k]


def all_reduce(x, groups, members):
    rows, cols = x.shape
    share = rows // groups
    return pl.pallas_call(
        lambda *refs: reduce_kernel(groups, members, *refs),
        out_shape=jax.ShapeDtypeStruct(x.shape, x.dtype),
        in_specs=[pl.BlockSpec(memory_space=pltpu.VMEM)],
        out_specs=pl.BlockSpec(memory_space=pltpu.VMEM),
        scratch_shapes=[
            pltpu.VMEM((groups, share, cols), jnp.float32),
            pltpu.VMEM((members, share, cols), jnp.float32),
            pltpu.VMEM((groups, share, cols), jnp.float32),
            pltpu.SemaphoreType.DMA((6, max(groups, members) - 1)),
        ],
        compiler_params=params(collective_id=0, has_side_effects=True),
        cost_estimate=cost(1_000_000, 4_000_000),
    )(x)


def sorted_by(key, *values):
    ids = jnp.arange(key.shape[0], dtype=jnp.int32)
    ahead = (key[None, :] < key[:, None]) | (
        (key[None, :] == key[:, None]) & (ids[None, :] < ids[:, None])
    )
    rank = jnp.sum(ahead, axis=1, dtype=jnp.int32)
    hit = rank[None, :] == ids[:, None]
    return [jnp.sum(jnp.where(hit, value[None, :], 0), axis=1) for value in (ids, *values)]


def per_device(
    hidden,
    initial,
    weight,
    grp_vals,
    grp_row,
    grp_col,
    bnd_vals,
    bnd_src,
    bnd_dst,
    bnd_row,
    cotangent,
):
    blk = grp_vals.shape[1]
    nodes, feat = hidden.shape
    nb = nodes // blk
    devices = lax.axis_size(AXES)
    groups, members = lax.axis_size("grp"), lax.axis_size("mem")
    count = bnd_vals.shape[0]
    blocks = hidden.reshape(nb, blk, feat)

    target = bnd_dst[:, 0]
    ids = jnp.arange(count, dtype=jnp.int32)
    place = jnp.sum(
        (target[:, None] == target[None, :]) & (ids[None, :] < ids[:, None]),
        axis=1,
        dtype=jnp.int32,
    )
    slot = target * 2 + place
    out_rows = jnp.max(
        jnp.where(
            slot[None, :] == jnp.arange(2 * devices, dtype=jnp.int32)[:, None],
            bnd_row[None, :],
            -1,
        ),
        axis=1,
    )
    in_rows = lax.all_to_all(
        out_rows.reshape(devices, 2), AXES, split_axis=0, concat_axis=0, tiled=True
    ).reshape(-1)
    table = lax.all_gather(blocks, "mem", axis=0, tiled=True)
    outgoing = partials(slot, bnd_src, bnd_vals, blocks, devices)
    edge_order, edge_row, edge_col = sorted_by(grp_col, grp_row, grp_col)
    empty = in_rows < 0
    key = jnp.where(empty, nb, in_rows)
    slot_order, slot_row = sorted_by(key, key)
    filled = jnp.sum(~empty, dtype=jnp.int32)[None]
    scalars = (
        slot_order,
        slot_row,
        filled,
        grp_row,
        grp_col,
        edge_order,
        edge_row,
        edge_col,
    )
    outgoing, table, scalars = lax.optimization_barrier((outgoing, table, scalars))
    incoming = lax.all_to_all(
        outgoing.reshape(devices, 2 * blk, feat), AXES, split_axis=0, concat_axis=0, tiled=True
    )
    output, term, local_weight = core(
        scalars,
        incoming.reshape(2 * devices, blk, feat),
        table,
        grp_vals,
        initial,
        cotangent,
        weight,
        nb,
    )
    grad_hidden = lax.psum_scatter(term, "mem", scatter_dimension=0, tiled=True)
    grad_weight = all_reduce(local_weight, groups, members) * (
        0.5 / math.sqrt(nodes * devices)
    )
    return output, grad_weight, grad_hidden.reshape(nodes, feat)


def solution(mesh):
    return jax.shard_map(
        per_device,
        mesh=mesh,
        in_specs=(
            P(AXES, None),
            P(AXES, None),
            P(),
            P(AXES, None, None),
            P(AXES),
            P(AXES),
            P(AXES, None, None),
            P(AXES),
            P(AXES, None),
            P(AXES),
            P(AXES, None),
        ),
        out_specs=(P(AXES, None), P(), P(AXES, None)),
        check_vma=False,
    )
```

```python
import math

import jax
import jax.numpy as jnp
from jax import lax
from jax.experimental import pallas as pl
from jax.experimental.pallas import tpu as pltpu
from jax.sharding import PartitionSpec as P

AXES = ("grp", "mem")
MESH = pl.DeviceIdType.MESH
VMEM_LIMIT = 56 * 1024 * 1024
BATCH = 8


def params(**kw):
    return pltpu.CompilerParams(vmem_limit_bytes=VMEM_LIMIT, **kw)


def full(shape):
    return pl.BlockSpec(shape, lambda *_: (0,) * len(shape))


def cost(flops, moved):
    return pl.CostEstimate(flops=flops, bytes_accessed=moved, transcendentals=0)


def partial_kernel(slot_ref, src_ref, vals_ref, hid_ref, out_ref, stage, sem):
    step = pl.program_id(0)
    half = lax.rem(step, 2)
    per_step = vals_ref.shape[0]

    def drain(which):
        for i in range(per_step):
            pltpu.make_async_copy(stage.at[which, i], out_ref.at[0], sem.at[which, i]).wait()

    @pl.when(step >= 2)
    def _():
        drain(half)

    for i in range(per_step):
        edge = step * per_step + i
        stage[half, i] = jnp.dot(
            vals_ref[i], hid_ref[src_ref[edge]], preferred_element_type=jnp.float32
        ).astype(stage.dtype)
    for i in range(per_step):
        edge = step * per_step + i
        pltpu.make_async_copy(
            stage.at[half, i], out_ref.at[slot_ref[edge]], sem.at[half, i]
        ).start()

    @pl.when(step == pl.num_programs(0) - 1)
    def _():
        drain(1 - half)
        drain(half)


def partials(slot, bnd_src, bnd_vals, blocks, devices):
    count, blk, _ = bnd_vals.shape
    nb, _, feat = blocks.shape
    per_step = 16
    assert count % per_step == 0 and count >= 2 * per_step
    return pl.pallas_call(
        partial_kernel,
        grid_spec=pltpu.PrefetchScalarGridSpec(
            num_scalar_prefetch=2,
            grid=(count // per_step,),
            in_specs=[
                pl.BlockSpec((per_step, blk, blk), lambda i, *_: (i, 0, 0)),
                full(blocks.shape),
            ],
            out_specs=pl.BlockSpec(memory_space=pl.ANY),
            scratch_shapes=[
                pltpu.VMEM((2, per_step, blk, feat), jnp.bfloat16),
                pltpu.SemaphoreType.DMA((2, per_step)),
            ],
        ),
        out_shape=jax.ShapeDtypeStruct((devices * 2, blk, feat), jnp.bfloat16),
        compiler_params=params(),
        cost_estimate=cost(2 * count * blk * blk * feat, 3 * count * blk * feat),
    )(slot, bnd_src, bnd_vals, blocks)


def core_kernel(
    slot_order,
    slot_row,
    filled,
    grp_row,
    grp_col,
    edge_order,
    edge_row,
    edge_col,
    inc_hbm,
    table_hbm,
    vals_hbm,
    initial_hbm,
    cot_hbm,
    w_ref,
    out_hbm,
    term_hbm,
    gw_ref,
    ring,
    table,
    vals,
    initial,
    cot,
    acc,
    running,
    out,
    gmix,
    term,
    mixed_all,
    gpre_all,
    mw,
    ring_sem,
    table_sem,
    vals_sem,
    in_sem,
    out_sem,
    term_sem,
):
    nb, blk, feat = gmix.shape
    depth = ring_sem.shape[0] // BATCH
    chunks = vals_sem.shape[0]
    per_chunk = vals.shape[0] // chunks
    batches = (filled[0] + BATCH - 1) // BATCH

    def fetch(batch, i):
        at = lax.rem(batch, depth) * BATCH + i
        return pltpu.make_async_copy(
            inc_hbm.at[slot_order[batch * BATCH + i]], ring.at[at], ring_sem.at[at]
        )

    def fetch_batch(batch):
        @pl.when(batch < batches)
        def _():
            for i in range(BATCH):
                fetch(batch, i).start()

    for batch in range(depth):
        fetch_batch(batch)
    table_copy = pltpu.make_async_copy(table_hbm, table, table_sem)
    table_copy.start()

    def vals_copy(chunk):
        at = pl.ds(chunk * per_chunk, per_chunk)
        return pltpu.make_async_copy(vals_hbm.at[at], vals.at[at], vals_sem.at[chunk])

    def start_vals(chunk, _):
        vals_copy(chunk).start()
        return 0

    lax.fori_loop(0, chunks, start_vals, 0)
    initial_copy = pltpu.make_async_copy(initial_hbm, initial, in_sem.at[0])
    cot_copy = pltpu.make_async_copy(cot_hbm, cot, in_sem.at[1])
    initial_copy.start()
    cot_copy.start()

    def zero_acc(j, _):
        acc[j] = jnp.zeros(acc.shape[1:], acc.dtype)
        return 0

    def zero_term(j, _):
        term[j] = jnp.zeros(term.shape[1:], term.dtype)
        return 0

    lax.fori_loop(0, nb, zero_acc, 0)
    lax.fori_loop(0, term.shape[0], zero_term, 0)
    eye = lax.broadcasted_iota(jnp.int32, (feat, feat), 0) == lax.broadcasted_iota(
        jnp.int32, (feat, feat), 1
    )
    mw[...] = (
        jnp.where(eye, 0.5, 0.0).astype(jnp.float32) + 0.5 * w_ref[...].astype(jnp.float32)
    ).astype(jnp.bfloat16)

    def follows(key, at):
        return (key[at] == key[jnp.maximum(at - 1, 0)]).astype(jnp.float32)

    def add_batch(batch, _):
        for i in range(BATCH):
            fetch(batch, i).wait()
        total = running[...]
        for i in range(BATCH):
            at = batch * BATCH + i
            total = total * follows(slot_row, at) + ring[
                lax.rem(batch, depth) * BATCH + i
            ].astype(jnp.float32)
            acc[slot_row[at]] = total
        running[...] = total
        fetch_batch(batch + depth)
        return 0

    running[...] = jnp.zeros_like(running)
    lax.fori_loop(0, batches, add_batch, 0)
    table_copy.wait()

    def forward(chunk, _):
        vals_copy(chunk).wait()
        for i in range(per_chunk):
            b = chunk * per_chunk + i
            acc[grp_row[b]] += jnp.dot(
                vals[b], table[grp_col[b]], preferred_element_type=jnp.float32
            )
        return 0

    lax.fori_loop(0, chunks, forward, 0)
    initial_copy.wait()
    cot_copy.wait()
    wide = 4

    def dense(j, _):
        at = pl.ds(pl.multiple_of(j * wide * blk, wide * blk), wide * blk)
        summed = acc[pl.ds(j * wide, wide)].reshape(wide * blk, feat)
        mixed = (0.9 * summed + 0.1 * initial[at, :].astype(jnp.float32)).astype(jnp.bfloat16)
        pre = jnp.dot(mixed, mw[...], preferred_element_type=jnp.float32)
        sig = jax.nn.sigmoid(pre)
        out[at, :] = (pre * sig).astype(jnp.bfloat16)
        gpre = (cot[at, :].astype(jnp.float32) * sig * (1.0 + pre * (1.0 - sig))).astype(
            jnp.bfloat16
        )
        mixed_all[at, :] = mixed
        gpre_all[at, :] = gpre
        gmix[pl.ds(j * wide, wide)] = (
            lax.dot_general(
                gpre, mw[...], (((1,), (1,)), ((), ())), preferred_element_type=jnp.float32
            )
            .astype(jnp.bfloat16)
            .reshape(wide, blk, feat)
        )
        return 0

    lax.fori_loop(0, nb // wide, dense, 0)
    out_copy = pltpu.make_async_copy(out, out_hbm, out_sem)
    out_copy.start()
    gw_ref[...] = lax.dot_general(
        mixed_all[...], gpre_all[...], (((0,), (0,)), ((), ())), preferred_element_type=jnp.float32
    )

    def send_term(c, _):
        pltpu.make_async_copy(term.at[c], term_hbm.at[c], term_sem).start()
        return 0

    running[...] = jnp.zeros_like(running)

    def backward(chunk, sent):
        total = running[...]
        for i in range(per_chunk):
            b = chunk * per_chunk + i
            col = edge_col[b]
            total = total * follows(edge_col, b) + lax.dot_general(
                vals[edge_order[b]],
                gmix[edge_row[b]],
                (((0,), (0,)), ((), ())),
                preferred_element_type=jnp.float32,
            )
            term[col] = (0.9 * total).astype(term.dtype)
        running[...] = total
        past = edge_col[chunk * per_chunk + per_chunk - 1]
        lax.fori_loop(sent, past, send_term, 0)
        return past

    sent = lax.fori_loop(0, chunks, backward, jnp.int32(0))
    lax.fori_loop(sent, term.shape[0], send_term, 0)
    out_copy.wait()
    pltpu.make_async_copy(term, term_hbm, term_sem).wait()


def core(scalars, incoming, table, grp_vals, initial, cotangent, weight, nb):
    count, blk, _ = grp_vals.shape
    nodes, feat = initial.shape
    ring, chunks = 16 * BATCH, 4
    assert count % chunks == 0 and incoming.shape[0] % BATCH == 0
    smem = pl.BlockSpec(memory_space=pltpu.SMEM)
    hbm = pl.BlockSpec(memory_space=pl.ANY)
    vmem = pl.BlockSpec(memory_space=pltpu.VMEM)
    bf16, dma = jnp.bfloat16, pltpu.SemaphoreType.DMA
    return pl.pallas_call(
        core_kernel,
        in_specs=[smem] * len(scalars) + [hbm] * 5 + [vmem],
        out_specs=[hbm, hbm, vmem],
        out_shape=[
            jax.ShapeDtypeStruct((nodes, feat), bf16),
            jax.ShapeDtypeStruct(table.shape, bf16),
            jax.ShapeDtypeStruct((feat, feat), jnp.float32),
        ],
        scratch_shapes=[
            pltpu.VMEM((ring, blk, feat), bf16),
            pltpu.VMEM(table.shape, bf16),
            pltpu.VMEM(grp_vals.shape, bf16),
            pltpu.VMEM((nodes, feat), bf16),
            pltpu.VMEM((nodes, feat), bf16),
            pltpu.VMEM((nb + 1, blk, feat), jnp.float32),
            pltpu.VMEM((blk, feat), jnp.float32),
            pltpu.VMEM((nodes, feat), bf16),
            pltpu.VMEM((nb, blk, feat), bf16),
            pltpu.VMEM(table.shape, bf16),
            pltpu.VMEM((nodes, feat), bf16),
            pltpu.VMEM((nodes, feat), bf16),
            pltpu.VMEM((feat, feat), bf16),
            dma((ring,)),
            dma,
            dma((chunks,)),
            dma((2,)),
            dma,
            dma,
        ],
        compiler_params=params(),
        cost_estimate=cost(4 * count * blk * blk * feat + 6 * nodes * feat * feat, 60_000_000),
    )(*scalars, incoming, table, grp_vals, initial, cotangent, weight)


def reduce_kernel(groups, members, x_ref, out_ref, part, whole, done, sems):
    g, m = lax.axis_index("grp"), lax.axis_index("mem")
    rows = part.shape[1]
    barrier = pltpu.get_barrier_semaphore()
    mates = [lax.rem(m + k, members) for k in range(1, members)]
    peers = [lax.rem(g + k, groups) for k in range(1, groups)]
    for mate in mates:
        pl.semaphore_signal(barrier, inc=1, device_id=(g, mate), device_id_type=MESH)
    for peer in peers:
        pl.semaphore_signal(barrier, inc=1, device_id=(peer, m), device_id_type=MESH)
    pl.semaphore_wait(barrier, members + groups - 2)

    def exchange(stage, targets, source, target):
        copies = []
        for k, (device, src) in enumerate(zip(targets, source)):
            copies.append(
                pltpu.make_async_remote_copy(
                    src,
                    target,
                    sems.at[2 * stage, k],
                    sems.at[2 * stage + 1, k],
                    device_id=device,
                    device_id_type=MESH,
                )
            )
            copies[-1].start()
        return copies

    def at(index):
        return pl.ds(pl.multiple_of(index * rows, rows), rows)

    def total(buffer):
        result = buffer[0]
        for k in range(1, buffer.shape[0]):
            result = result + buffer[k]
        return result

    far = [(peer, m) for peer in peers]
    copies = exchange(0, far, [x_ref.at[at(peer)] for peer in peers], part.at[g])
    part[g] = x_ref[at(g), :]
    for copy in copies:
        copy.wait()
    whole[m] = total(part)
    for copy in exchange(1, [(g, mate) for mate in mates], [whole.at[m]] * len(mates), whole.at[m]):
        copy.wait()
    done[g] = total(whole)
    for copy in exchange(2, far, [done.at[g]] * len(far), done.at[g]):
        copy.wait()
    for k in range(groups):
        out_ref[k * rows : (k + 1) * rows, :] = done[k]


def all_reduce(x, groups, members):
    rows, cols = x.shape
    share = rows // groups
    return pl.pallas_call(
        lambda *refs: reduce_kernel(groups, members, *refs),
        out_shape=jax.ShapeDtypeStruct(x.shape, x.dtype),
        in_specs=[pl.BlockSpec(memory_space=pltpu.VMEM)],
        out_specs=pl.BlockSpec(memory_space=pltpu.VMEM),
        scratch_shapes=[
            pltpu.VMEM((groups, share, cols), jnp.float32),
            pltpu.VMEM((members, share, cols), jnp.float32),
            pltpu.VMEM((groups, share, cols), jnp.float32),
            pltpu.SemaphoreType.DMA((6, max(groups, members) - 1)),
        ],
        compiler_params=params(collective_id=0, has_side_effects=True),
        cost_estimate=cost(1_000_000, 4_000_000),
    )(x)


def sorted_by(key, *values):
    ids = jnp.arange(key.shape[0], dtype=jnp.int32)
    ahead = (key[None, :] < key[:, None]) | (
        (key[None, :] == key[:, None]) & (ids[None, :] < ids[:, None])
    )
    rank = jnp.sum(ahead, axis=1, dtype=jnp.int32)
    hit = rank[None, :] == ids[:, None]
    return [jnp.sum(jnp.where(hit, value[None, :], 0), axis=1) for value in (ids, *values)]


def per_device(
    hidden,
    initial,
    weight,
    grp_vals,
    grp_row,
    grp_col,
    bnd_vals,
    bnd_src,
    bnd_dst,
    bnd_row,
    cotangent,
):
    blk = grp_vals.shape[1]
    nodes, feat = hidden.shape
    nb = nodes // blk
    devices = lax.axis_size(AXES)
    groups, members = lax.axis_size("grp"), lax.axis_size("mem")
    count = bnd_vals.shape[0]
    blocks = hidden.reshape(nb, blk, feat)

    target = bnd_dst[:, 0]
    ids = jnp.arange(count, dtype=jnp.int32)
    place = jnp.sum(
        (target[:, None] == target[None, :]) & (ids[None, :] < ids[:, None]),
        axis=1,
        dtype=jnp.int32,
    )
    slot = target * 2 + place
    out_rows = jnp.max(
        jnp.where(
            slot[None, :] == jnp.arange(2 * devices, dtype=jnp.int32)[:, None],
            bnd_row[None, :],
            -1,
        ),
        axis=1,
    )
    in_rows = lax.all_to_all(
        out_rows.reshape(devices, 2), AXES, split_axis=0, concat_axis=0, tiled=True
    ).reshape(-1)
    table = lax.all_gather(blocks, "mem", axis=0, tiled=True)
    outgoing = partials(slot, bnd_src, bnd_vals, blocks, devices)
    edge_order, edge_row, edge_col = sorted_by(grp_col, grp_row, grp_col)
    empty = in_rows < 0
    key = jnp.where(empty, nb, in_rows)
    slot_order, slot_row = sorted_by(key, key)
    filled = jnp.sum(~empty, dtype=jnp.int32)[None]
    scalars = (
        slot_order,
        slot_row,
        filled,
        grp_row,
        grp_col,
        edge_order,
        edge_row,
        edge_col,
    )
    outgoing, table, scalars = lax.optimization_barrier((outgoing, table, scalars))
    incoming = lax.all_to_all(
        outgoing.reshape(devices, 2 * blk, feat), AXES, split_axis=0, concat_axis=0, tiled=True
    )
    output, term, local_weight = core(
        scalars,
        incoming.reshape(2 * devices, blk, feat),
        table,
        grp_vals,
        initial,
        cotangent,
        weight,
        nb,
    )
    grad_hidden = lax.psum_scatter(term, "mem", scatter_dimension=0, tiled=True)
    grad_weight = all_reduce(local_weight, groups, members) * (
        0.5 / math.sqrt(nodes * devices)
    )
    return output, grad_weight, grad_hidden.reshape(nodes, feat)


def solution(mesh):
    return jax.shard_map(
        per_device,
        mesh=mesh,
        in_specs=(
            P(AXES, None),
            P(AXES, None),
            P(),
            P(AXES, None, None),
            P(AXES),
            P(AXES),
            P(AXES, None, None),
            P(AXES),
            P(AXES, None),
            P(AXES),
            P(AXES, None),
        ),
        out_specs=(P(AXES, None), P(), P(AXES, None)),
        check_vma=False,
    )
```
